32 devices in a mesh: occ: 4 (over z), virt: 8 (over y, x, core).
Axes of the slice: x: 2, y: 2, z: 4, core: 2. Of those that a mesh axis runs over, the one named last changes fastest.
Arguments:
- basis_integrals: bfloat16 [16, 1280, 2048], P(None, 'virt', 'occ'), may hold values from -2 to 2
- group_sizes: int32 [4], replicated, may hold values from 1 to 6, 16 in all
- orbital_order: int32 [16], replicated, may hold values from 0 to 15, each once
- eps_occ: float32 [16], replicated, may hold values from -1.5 to -0.3
- eps_vir: float32 [1280], replicated, may hold values from 0.2 to 2.5
Outputs:
- density: bfloat16 [4, 6, 1280, 2048], P('occ', None, 'virt')
The draws below stay inside these ranges and needn't reach their ends.
Inputs may be any that keep to these rules, and one draw needn't show every extreme that they name: `group_sizes`: each group holds 1 to 6 orbitals, 16 together, and some group holds exactly 6. `orbital_order`: each window orbital appears once.
All inputs are finite; a program needn't handle non-finite values.
Results may differ from the reference program's by a relative error of at most 0.0034.
Values may be sent and summed in bfloat16 or wider, within the bound.
No kernel may reach another device: no remote copies, remote signals or barrier semaphores. Data moves between devices by JAX's collectives and lax.ppermute only.
A program may use at most 128 MiB of HBM per device.

```python
import math
import jax
import jax.numpy as jnp
import numpy as np
from jax import lax

NVIR = 1280
NAUX = 2048
CAP = 6
NW = 16
N_OCC = 4


def block_scale(rng, extent, split, low, high):
    loudness, own = 1.0, jax.random.fold_in(rng, 6)
    for dim, parts in split:
        steps = jnp.exp(jax.random.uniform(jax.random.fold_in(own, dim), (parts,), jnp.float32, low / len(split), high / len(split)))
        loudness = loudness * jnp.repeat(steps, extent[dim] // parts).reshape([-1 if axis == dim else 1 for axis in range(len(extent))])
    return loudness


def profile(number_of, total, bound, slope):
    loads = [(1 << 20) // math.isqrt(grade ** slope) + 1 for grade in range(2, number_of + 1)]
    surplus, counts = total - bound - (number_of - 1), [1] * (number_of - 1)
    while surplus > 0:
        free = [i for i in range(number_of - 1) if counts[i] < bound]
        pool, remaining = sum([loads[i] for i in free]), surplus
        for i in free:
            extra = min(bound - counts[i], max(1, remaining * loads[i] // pool), surplus)
            counts[i] = counts[i] + extra
            surplus = surplus - extra
    return np.array([bound] + counts)


def uneven_parts(own_key, amount, total, reach, skew):
    if amount == 2:
        one = jax.random.randint(own_key, (), max(1, total - reach), min(reach, total - 1) + 1)
        return jnp.stack([one, total - one])
    lengths = jnp.asarray(profile(amount, total, reach, skew), jnp.int32)
    pairs = (amount - 1) // 2
    donor, receiver = lengths[1:1 + 2 * pairs:2], lengths[2:2 + 2 * pairs:2]
    room = jnp.minimum(donor - 1, reach - receiver)
    passed = jax.random.randint(jax.random.fold_in(own_key, 1), (pairs,), 0, 1 << 20) % (room + 1)
    lengths = lengths.at[1:1 + 2 * pairs:2].set(donor - passed).at[2:2 + 2 * pairs:2].set(receiver + passed)
    return lengths[jax.random.permutation(jax.random.fold_in(own_key, 2), amount)]


def scatter_about(own_key, extent, deviation, limit, cuts=(), kind=jnp.bfloat16):
    drawn = deviation * jax.random.normal(own_key, extent, jnp.float32)
    if cuts:
        drawn = drawn * block_scale(own_key, extent, cuts, -0.22, 0.18)
    return jnp.clip(drawn, -limit, limit).astype(kind)


def setup_inputs(seed: int = 0) -> dict:
    key_of = jax.random.split(jax.random.key(seed), 6)
    basis_integrals = scatter_about(key_of[0], (NW, NVIR, NAUX), (NAUX ** -0.25), 2.0, ((1, 8), (2, 4)))
    group_sizes = uneven_parts(key_of[1], N_OCC, NW, CAP, 1).astype(jnp.int32)
    orbital_order = jax.random.permutation(key_of[2], NW).astype(jnp.int32)
    eps_occ = jnp.clip(jax.random.uniform(key_of[3], (NW,), jnp.float32, -1.5, -0.3), -1.5, -0.3)
    eps_vir = jnp.clip(jax.random.uniform(key_of[4], (NVIR,), jnp.float32, 0.2, 2.5), 0.2, 2.5)
    return dict(basis_integrals=basis_integrals, group_sizes=group_sizes, orbital_order=orbital_order, eps_occ=eps_occ, eps_vir=eps_vir)


def reference(basis_integrals, group_sizes, orbital_order, eps_occ, eps_vir):
    slot_index = jnp.arange(CAP, dtype=jnp.int32)
    offsets = (jnp.cumsum(group_sizes) - group_sizes).astype(jnp.int32)
    occupied = slot_index[None, :] < group_sizes[:, None]
    position = jnp.clip(offsets[:, None] + slot_index[None, :], 0, NW - 1).astype(jnp.int32)
    orbital = jnp.where(occupied, orbital_order[position], 0).astype(jnp.int32)

    def one_group(group_args):
        orbitals, alive = group_args
        slot_mask = jnp.where(alive, 1.0, 0.0).astype(jnp.bfloat16)
        selected = basis_integrals[orbitals] * slot_mask[:, None, None]
        flattened = selected.reshape(CAP * NVIR, NAUX).astype(jnp.float32)
        coulomb = jnp.dot(flattened, flattened.T, precision=lax.Precision.HIGHEST)
        occ_energy = jnp.where(alive, eps_occ[orbitals], jnp.float32(0.0))
        row_gap = (occ_energy[:, None] - eps_vir[None, :]).reshape(-1)
        amplitude = coulomb / (row_gap[:, None] + row_gap[None, :])
        amp_four = amplitude.reshape(CAP, NVIR, CAP, NVIR)
        combined = (2.0 * amp_four - amp_four.transpose(2, 1, 0, 3)).reshape(CAP * NVIR, CAP * NVIR)
        combined = combined.astype(jnp.bfloat16).astype(jnp.float32)
        density = jnp.dot(combined, flattened, precision=lax.Precision.HIGHEST)
        return density.reshape(CAP, NVIR, NAUX).astype(jnp.bfloat16)

    return lax.map(one_group, (orbital, occupied))
```

```python
import functools

import jax
import jax.numpy as jnp
from jax import lax
from jax.experimental import pallas as pl
from jax.experimental.pallas import tpu as pltpu
from jax.sharding import PartitionSpec as P

CAP = 6
LANES = 256
VMEM_LIMIT = 62 << 20
SMALL = pl.CostEstimate(flops=1 << 10, bytes_accessed=1 << 10, transcendentals=0)
ANY = pl.BlockSpec(memory_space=pl.ANY)
VMEM = pl.BlockSpec(memory_space=pltpu.VMEM)
SMEM = pl.BlockSpec(memory_space=pltpu.SMEM)


def group_slots(sizes, order, group, n_groups):
    offset = jnp.int32(0)
    count = jnp.int32(0)
    for other in range(n_groups):
        offset = offset + jnp.where(other < group, sizes[other], 0)
        count = count + jnp.where(other == group, sizes[other], 0)
    last = order.shape[0] - 1
    return [
        (order[jnp.minimum(offset + slot, last)], slot < count) for slot in range(CAP)
    ]


def stage_kernel(n_occ, cuts, me, sizes, order, basis, *refs):
    outs, (token, held, read, sent) = refs[: 1 + len(cuts)], refs[-4:]
    token[...] = jnp.zeros(token.shape, token.dtype)
    reads = []
    for mask in range(n_occ):
        for slot, (orbital, live) in enumerate(
            group_slots(sizes, order, me[0] ^ mask, n_occ)
        ):
            copy = pltpu.make_async_copy(
                basis.at[orbital], held.at[mask, slot], read.at[mask * CAP + slot]
            )
            copy.start()
            reads.append((copy, live, mask, slot))
    for copy, live, mask, slot in reads:
        copy.wait()

        @pl.when(jnp.logical_not(live))
        def _():
            held[mask, slot] = jnp.zeros(held.shape[2:], held.dtype)

    copies = [pltpu.make_async_copy(held.at[0], outs[0], sent.at[0])]
    low = 0
    for c, rows in enumerate(cuts):
        for mask in range(n_occ):
            index = 1 + c * n_occ + mask
            copies.append(
                pltpu.make_async_copy(
                    held.at[mask, :, pl.ds(low, rows)], outs[1 + c].at[me[0] ^ mask], sent.at[index]
                )
            )
        low += rows
    for copy in copies:
        copy.start()
    for copy in copies:
        copy.wait()


def stage(basis, me, sizes, order, n_occ, cuts):
    width, aux = basis.shape[1:]
    n_sends = len(cuts)
    return pl.pallas_call(
        functools.partial(stage_kernel, n_occ, cuts),
        out_shape=[jax.ShapeDtypeStruct((CAP, width, aux), basis.dtype)]
        + [
            jax.ShapeDtypeStruct((n_occ, CAP, rows, aux), basis.dtype)
            for rows in cuts
        ]
        + [jax.ShapeDtypeStruct((8, 128), jnp.float32)],
        in_specs=[SMEM, SMEM, SMEM, ANY],
        out_specs=[ANY] * (1 + n_sends) + [VMEM],
        scratch_shapes=[
            pltpu.VMEM((n_occ, CAP, width, aux), basis.dtype),
            pltpu.SemaphoreType.DMA((n_occ * CAP,)),
            pltpu.SemaphoreType.DMA((1 + n_occ * n_sends,)),
        ],
        compiler_params=pltpu.CompilerParams(vmem_limit_bytes=VMEM_LIMIT),
        cost_estimate=SMALL,
    )(me, sizes, order, basis)


def gate(token, needs=(), gives=()):
    operands = [token, *gives, *needs]
    kept = 1 + len(gives)
    done = pl.pallas_call(
        lambda *refs: None,
        out_shape=[jax.ShapeDtypeStruct(x.shape, x.dtype) for x in operands[:kept]],
        in_specs=[ANY] * len(operands),
        out_specs=[ANY] * kept,
        input_output_aliases={i: i for i in range(kept)},
        compiler_params=pltpu.CompilerParams(vmem_limit_bytes=VMEM_LIMIT),
        cost_estimate=SMALL,
    )(*operands)
    return done[0], done[1:]


def join_kernel(n_occ, parts, me, token_in, got, token, *refs):
    outs, (held, read, sent) = refs[:parts], refs[parts:]
    reads = [
        pltpu.make_async_copy(got.at[me[0] ^ mask], held.at[mask - 1], read.at[mask])
        for mask in range(1, n_occ)
    ]
    width = held.shape[2] // parts
    sends = [
        pltpu.make_async_copy(held.at[:, :, pl.ds(i * width, width)], outs[i], sent.at[i])
        for i in range(parts)
    ]
    for copy in reads:
        copy.start()
    for copy in reads:
        copy.wait()
    for copy in sends:
        copy.start()
    for copy in sends:
        copy.wait()


def join(token, me, got, parts):
    n_occ, cap, rows, aux = got.shape
    shape = jax.ShapeDtypeStruct((n_occ - 1, cap, rows // parts, aux), got.dtype)
    done = pl.pallas_call(
        functools.partial(join_kernel, n_occ, parts),
        out_shape=[jax.ShapeDtypeStruct(token.shape, token.dtype)] + [shape] * parts,
        in_specs=[SMEM, ANY, ANY],
        out_specs=[ANY] * (1 + parts),
        scratch_shapes=[
            pltpu.VMEM((n_occ - 1, cap, rows, aux), got.dtype),
            pltpu.SemaphoreType.DMA((n_occ,)),
            pltpu.SemaphoreType.DMA((parts,)),
        ],
        input_output_aliases={1: 0},
        compiler_params=pltpu.CompilerParams(vmem_limit_bytes=VMEM_LIMIT),
        cost_estimate=SMALL,
    )(me, token, got)
    return done[0], done[1:]


def runs(flags, low, high):
    out = []
    for p in range(low, high):
        if out and flags[p] == out[-1][2]:
            out[-1] = (out[-1][0], p + 1, flags[p])
        else:
            out.append((p, p + 1, flags[p]))
    return out


def density_kernel(
    n_occ, n_blocks, n_parts, jobs, held, last, me, sizes, order, eps_occ, va, vb, *refs
):
    refs = list(refs)
    refs.pop(0)
    first_blocks = [refs.pop(0) for _ in range(n_blocks)]
    units = sorted({unit for _, _, chosen in jobs for unit in chosen})
    row_parts = range(min(low for low, _, _ in jobs), max(high for _, high, _ in jobs))
    col_blocks = {unit: [refs.pop(0) for _ in range(n_blocks)] for unit in units}
    own_parts = {
        p: col_blocks[p][0] if p in units else refs.pop(0) for p in row_parts
    }
    before = refs.pop(0) if any(held) else None
    refs.pop(0)
    out, rows, cols, kbuf, abuf, total, result, sems = refs
    width, aux = rows.shape[2], rows.shape[3]
    part = width // n_parts
    n_copies = 0

    def copy(source, target):
        nonlocal n_copies
        made = pltpu.make_async_copy(source, target, sems.at[n_copies])
        made.start()
        n_copies += 1
        return made

    here = pl.ds(row_parts[0] * part, len(row_parts) * part)
    row_copies = [copy(first_blocks[0].at[:, here], rows.at[0, :, here])]
    for p in row_parts:
        row_copies.append(
            copy(own_parts[p], rows.at[pl.ds(1, n_occ - 1), :, pl.ds(p * part, part)])
        )
    col_copies = {}
    for index, unit in enumerate(units):
        copies = []
        for b in range(n_blocks):
            copies.append(
                copy(
                    first_blocks[b].at[:, pl.ds(unit * part, part)],
                    cols.at[index, 0, :, pl.ds(b * part, part)],
                )
            )
            copies.append(
                copy(
                    col_blocks[unit][b],
                    cols.at[index, pl.ds(1, n_occ - 1), :, pl.ds(b * part, part)],
                )
            )
        col_copies[unit] = copies
    total_copies = [
        copy(before.at[:, pl.ds(a * part, (b - a) * part)], total.at[:, pl.ds(a * part, (b - a) * part)])
        for a, b, flag in runs(held, 0, n_parts)
        if flag
    ]
    energy = []
    for orbital, live in group_slots(sizes, order, me[0], n_occ):
        energy.append(jnp.where(live, eps_occ[orbital], jnp.float32(0.0)))
    for made in row_copies:
        made.wait()

    def combine(low, n_rows, unit, at, i, j):
        step = 32 if n_rows % 32 == 0 else 16
        for r in range(0, n_rows, step):
            gap = (energy[i] + energy[j]) - (va[pl.ds(low + r, step), :] + vb[unit])
            inverse = pltpu.reciprocal(gap, approx=True)
            inverse = inverse * (2.0 - gap * inverse)
            upper = kbuf[j, pl.ds(i * n_rows + r, step), :]
            if i == j:
                abuf[pl.ds(i * n_rows + r, step), pl.ds(at + j * LANES, LANES)] = (
                    upper * inverse
                ).astype(abuf.dtype)
            else:
                lower = kbuf[i, pl.ds(j * n_rows + r, step), :]
                abuf[pl.ds(i * n_rows + r, step), pl.ds(at + j * LANES, LANES)] = (
                    (upper + upper - lower) * inverse
                ).astype(abuf.dtype)
                abuf[pl.ds(j * n_rows + r, step), pl.ds(at + i * LANES, LANES)] = (
                    (lower + lower - upper) * inverse
                ).astype(abuf.dtype)

    span = min(n_occ, max(1, 1024 // aux))
    flags = list(held)
    sent = []
    for number, (low, high, chosen) in enumerate(jobs):
        first_row, n_rows = low * part, (high - low) * part
        for slot, unit in enumerate(chosen):
            for made in col_copies.pop(unit, ()):
                made.wait()
            index = units.index(unit)
            for j in range(CAP + 1):
                if j < CAP:
                    left = jnp.concatenate(
                        [
                            rows[s, :, first_row : first_row + n_rows].reshape(CAP * n_rows, aux)
                            for s in range(n_occ)
                        ],
                        axis=1,
                    )
                    right = jnp.concatenate([cols[index, s, j] for s in range(n_occ)], axis=1)
                    kbuf[j, pl.ds(0, CAP * n_rows)] = lax.dot_general(
                        left, right, (((1,), (1,)), ((), ())), preferred_element_type=jnp.float32
                    )
                for i in range(j):
                    combine(first_row, n_rows, unit, slot * CAP * LANES, i, j - 1)
        if number == 0:
            for made in total_copies:
                made.wait()
        depth = len(chosen) * CAP * LANES
        for s in range(0, n_occ, span):
            lanes = pl.ds(s * aux, span * aux)
            right = jnp.concatenate(
                [
                    jnp.concatenate(
                        [cols[units.index(unit), t].reshape(CAP * LANES, aux) for unit in chosen],
                        axis=0,
                    )
                    for t in range(s, s + span)
                ],
                axis=1,
            )
            added = jnp.dot(
                abuf[pl.ds(0, CAP * n_rows), pl.ds(0, depth)], right, preferred_element_type=jnp.float32
            ).reshape(CAP, n_rows, span * aux)
            final = number == len(jobs) - 1
            for a, b, flag in runs(flags, low, high):
                where = pl.ds(a * part, (b - a) * part)
                piece = added[:, (a - low) * part : (b - low) * part]
                if flag:
                    piece = piece + total[:, where, lanes]
                if last and final:
                    result[:, where, lanes] = piece.astype(result.dtype)
                else:
                    total[:, where, lanes] = piece
            if final:
                if last:
                    for t in range(s, s + span):
                        place = pl.multiple_of((me[0] ^ t) * aux, aux)
                        sent.append(
                            copy(result.at[:, :, pl.ds(t * aux, aux)], out.at[:, :, pl.ds(place, aux)])
                        )
                else:
                    for a, b, flag in runs(
                        [f or low <= p < high for p, f in enumerate(flags)], 0, n_parts
                    ):
                        where = pl.ds(a * part, (b - a) * part)
                        if flag:
                            sent.append(
                                copy(total.at[:, where, lanes], out.at[:, where, lanes])
                            )
        flags = [f or low <= p < high for p, f in enumerate(flags)]
    for made in sent:
        made.wait()


def density(token, scalars, first_blocks, chunks, before, held, jobs, last):
    n_parts = len(held)
    n_blocks = len(first_blocks)
    width, aux = first_blocks[0].shape[1:]
    part = width // n_parts
    n_occ = chunks[0][0].shape[0] + 1
    naux = n_occ * aux
    units = sorted({unit for _, _, chosen in jobs for unit in chosen})
    row_parts = range(min(low for low, _, _ in jobs), max(high for _, high, _ in jobs))
    kept = jnp.bfloat16 if last else jnp.float32
    deepest = max(len(chosen) for _, _, chosen in jobs)
    tallest = max(high - low for low, high, _ in jobs) * part * CAP
    operands = [*scalars, token, *first_blocks]
    for unit in units:
        operands += chunks[unit]
    operands += [chunks[p][0] for p in row_parts if p not in units]
    operands += [before] if any(held) else []
    at = len(scalars)
    done = pl.pallas_call(
        functools.partial(density_kernel, n_occ, n_blocks, n_parts, jobs, held, last),
        out_shape=[
            jax.ShapeDtypeStruct(token.shape, token.dtype),
            jax.ShapeDtypeStruct((CAP, width, naux), kept),
        ],
        in_specs=[SMEM] * 4 + [VMEM] * 2 + [ANY] * (len(operands) - at),
        out_specs=[ANY] * 2,
        scratch_shapes=[
            pltpu.VMEM((n_occ, CAP, width, aux), jnp.bfloat16),
            pltpu.VMEM((len(units), n_occ, CAP, LANES, aux), jnp.bfloat16),
            pltpu.VMEM((CAP, tallest, LANES), jnp.float32),
            pltpu.VMEM((tallest, deepest * CAP * LANES), jnp.bfloat16),
            pltpu.VMEM((CAP, width, naux), jnp.float32),
            pltpu.VMEM((CAP, width, naux) if last else (1, 16, 128), jnp.bfloat16),
            pltpu.SemaphoreType.DMA((48 + 2 * n_blocks * len(units),)),
        ],
        input_output_aliases={at: 0},
        compiler_params=pltpu.CompilerParams(vmem_limit_bytes=VMEM_LIMIT),
        cost_estimate=SMALL,
    )(*operands)
    held = tuple(
        f or any(low <= p < high for low, high, _ in jobs) for p, f in enumerate(held)
    )
    return done[0], done[1], held


def on_device(basis, group_sizes, orbital_order, eps_occ, eps_vir):
    n_virt, n_occ = lax.axis_size("virt"), lax.axis_size("occ")
    me_occ, me_virt = lax.axis_index("occ"), lax.axis_index("virt")
    width, aux = basis.shape[1:]
    dims = (n_virt // 2).bit_length() - 1
    part = LANES // n_virt
    n_parts = width // part
    me = me_occ.reshape(1).astype(jnp.int32)
    n_own = 1 << dims

    def bit(dim, core):
        return 2 << ((dim + core) % dims)

    def hop(block, dim):
        pairs = [(d, d ^ bit(dim, d & 1)) for d in range(n_virt)]
        return lax.ppermute(block, "virt", pairs)

    def sibling(block):
        return lax.ppermute(block, "virt", [(d, d ^ 1) for d in range(n_virt)])

    def origin(mask, core):
        return sum(bit(dim, core) for dim in range(dims) if mask >> dim & 1)

    core = me_virt & 1
    origins = [
        me_virt ^ jnp.where(core == 0, origin(m, 0), origin(m, 1)) for m in range(n_own)
    ] + [
        me_virt ^ 1 ^ jnp.where(core == 0, origin(m, 1), origin(m, 0)) for m in range(n_own)
    ]
    by_owner = eps_vir.reshape(n_virt, n_parts, part)
    vb = by_owner[jnp.stack(origins)].transpose(1, 0, 2).reshape(n_parts, 1, LANES)
    va = lax.dynamic_slice_in_dim(eps_vir, me_virt * width, width).reshape(width, 1)
    scalars = (me, group_sizes, orbital_order, eps_occ, va, vb)

    z_parts = (1, 2, 2)
    *sends, token = stage(
        basis, *scalars[:3], n_occ, tuple(n * part for n in z_parts)
    )
    blocks = {}

    def spread(name, block):
        held = blocks[name] = [block] + [None] * (2 * n_own - 1)
        held[n_own] = sibling(block)
        for dim in range(dims):
            held[1 << dim] = hop(block, dim)

    def relay(token, name, level):
        held = blocks[name]
        arrived = [m for m in range(1, n_own) if m.bit_count() == level]
        token, gated = gate(token, (), [held[m] for m in arrived])
        for m, block in zip(arrived, gated):
            held[m] = block
        for m in arrived:
            for dim in range(m.bit_length(), dims):
                held[m | 1 << dim] = hop(held[m], dim)
        for m in arrived:
            held[n_own + m] = sibling(held[m])
        return token

    crossing = []
    n_chunks = len(z_parts)

    def cross(token, c):
        token, (gated,) = gate(token, (), (sends[1 + c],))
        crossing.append(lax.all_to_all(gated, "occ", 0, 0, tiled=True))
        return token

    for c in range(n_chunks):
        token = cross(token, c)
        if c == 0:
            spread("first", sends[0])
    token = relay(token, "first", 1)
    joined = []
    token, pieces = join(token, me, crossing[0], z_parts[0])
    joined += pieces
    spread(0, joined[0])
    for level in range(2, dims + 1):
        token = relay(token, "first", level)
    token = relay(token, 0, 1)
    token, pieces = join(token, me, crossing[1], z_parts[1])
    joined += pieces
    spread(1, joined[1])
    for level in range(2, dims + 1):
        token = relay(token, 0, level)
    total, held = None, (False,) * n_parts

    def add(jobs, last=False):
        nonlocal token, total, held
        units = sorted({unit for _, _, chosen in jobs for unit in chosen})
        chunks = [blocks[p] if p in blocks else [block] for p, block in enumerate(joined)]
        token, total, held = density(
            token, scalars, blocks["first"], chunks, total, held, jobs, last
        )

    n_early = len(joined)
    add([(0, n_early, (0,))])
    token = relay(token, 1, 1)
    token, (joined[2],) = gate(token, (), (joined[2],))
    spread(2, joined[2])
    for level in range(2, dims + 1):
        token = relay(token, 1, level)
    token, pieces = join(token, me, crossing[2], z_parts[2])
    joined += pieces
    token = relay(token, 2, 1)
    spread(3, joined[3])
    add([(n_early, n_parts, (0,)), (0, n_parts, (1,))])
    for level in range(2, dims + 1):
        token = relay(token, 2, level)
    token = relay(token, 3, 1)
    token, (joined[4],) = gate(token, (), (joined[4],))
    spread(4, joined[4])
    add([(0, n_parts, (2,))])
    for level in range(2, dims + 1):
        token = relay(token, 3, level)
    token = relay(token, 4, 1)
    add([(0, n_parts, (3,))])
    for level in range(2, dims + 1):
        token = relay(token, 4, level)
    add([(0, n_parts, (4,))], True)
    return total.reshape(1, CAP, width, n_occ * aux)


def solution(mesh):
    return jax.shard_map(
        on_device,
        mesh=mesh,
        in_specs=(P(None, "virt", "occ"), P(), P(), P(), P()),
        out_specs=P("occ", None, "virt", None),
        check_vma=False,
    )
```

```python
import functools

import jax
import jax.numpy as jnp
from jax import lax
from jax.experimental import pallas as pl
from jax.experimental.pallas import tpu as pltpu
from jax.sharding import PartitionSpec as P

CAP = 6
LANES = 256
VMEM_LIMIT = (64 << 20) - (512 << 10)
SMALL = pl.CostEstimate(flops=1 << 10, bytes_accessed=1 << 10, transcendentals=0)
ANY = pl.BlockSpec(memory_space=pl.ANY)
VMEM = pl.BlockSpec(memory_space=pltpu.VMEM)
SMEM = pl.BlockSpec(memory_space=pltpu.SMEM)


def group_slots(sizes, order, group, n_groups):
    offset = jnp.int32(0)
    count = jnp.int32(0)
    for other in range(n_groups):
        offset = offset + jnp.where(other < group, sizes[other], 0)
        count = count + jnp.where(other == group, sizes[other], 0)
    last = order.shape[0] - 1
    return [
        (order[jnp.minimum(offset + slot, last)], slot < count) for slot in range(CAP)
    ]


def stage_kernel(n_occ, low, high, with_own, split, me, sizes, order, basis, token_in, *refs):
    outs, own, (held, read, sent) = refs[1:-3], refs[-4], refs[-3:]
    reads = []
    copies = []
    rows = pl.ds(low, high - low)
    for mask in range(n_occ):
        whole = with_own and mask == 0
        for slot, (orbital, live) in enumerate(
            group_slots(sizes, order, me[0] ^ mask, n_occ)
        ):
            index = mask * CAP + slot
            if whole:
                copy = pltpu.make_async_copy(basis.at[orbital], held.at[0, slot], read.at[index])
            else:
                copy = pltpu.make_async_copy(
                    basis.at[orbital, rows], held.at[mask, slot, pl.ds(0, high - low)], read.at[index]
                )
            copy.start()
            reads.append((copy, live))
    for mask in range(n_occ):
        for slot in range(CAP):
            copy, live = reads[mask * CAP + slot]
            copy.wait()

            @pl.when(jnp.logical_not(live))
            def _():
                held[mask, slot] = jnp.zeros(held.shape[2:], held.dtype)

        if mask or not split:
            target = outs[mask - 1] if split else outs[0].at[me[0] ^ mask]
            copies.append(
                pltpu.make_async_copy(held.at[mask, :, pl.ds(0, high - low)], target, sent.at[mask])
            )
            copies[-1].start()
        if with_own and mask == 0:
            copies.append(pltpu.make_async_copy(held.at[0], own, sent.at[n_occ]))
            copies[-1].start()
    for copy in copies:
        copy.wait()


def stage(token, basis, me, sizes, order, n_occ, low, high, with_own=False, split=False):
    width, aux = basis.shape[1:]
    piece = (CAP, high - low, aux)
    shapes = [piece] * (n_occ - 1) if split else [(n_occ, *piece)]
    shapes += [(CAP, width, aux)] * with_own
    return pl.pallas_call(
        functools.partial(stage_kernel, n_occ, low, high, with_own, split),
        out_shape=[
            jax.ShapeDtypeStruct(token.shape, token.dtype),
            *[jax.ShapeDtypeStruct(shape, basis.dtype) for shape in shapes],
        ],
        in_specs=[SMEM, SMEM, SMEM, ANY, ANY],
        out_specs=[ANY] * (1 + len(shapes)),
        scratch_shapes=[
            pltpu.VMEM((n_occ, CAP, width if with_own else high - low, aux), basis.dtype),
            pltpu.SemaphoreType.DMA((n_occ * CAP,)),
            pltpu.SemaphoreType.DMA((1 + n_occ,)),
        ],
        input_output_aliases={4: 0},
        compiler_params=pltpu.CompilerParams(vmem_limit_bytes=VMEM_LIMIT),
        cost_estimate=SMALL,
    )(me, sizes, order, basis, token)


def gate(token, needs=(), gives=()):
    operands = [token, *gives, *needs]
    kept = 1 + len(gives)
    done = pl.pallas_call(
        lambda *refs: None,
        out_shape=[jax.ShapeDtypeStruct(x.shape, x.dtype) for x in operands[:kept]],
        in_specs=[ANY] * len(operands),
        out_specs=[ANY] * kept,
        input_output_aliases={i: i for i in range(kept)},
        compiler_params=pltpu.CompilerParams(vmem_limit_bytes=VMEM_LIMIT),
        cost_estimate=SMALL,
    )(*operands)
    return done[0], done[1:]


def join_kernel(n_occ, n_got, parts, me, token_in, *refs):
    got, outs, (held, read, sent) = refs[:n_got], refs[n_got + 1 : -3], refs[-3:]
    sources = got if n_got > 1 else [got[0].at[me[0] ^ mask] for mask in range(1, n_occ)]
    reads = [
        pltpu.make_async_copy(source, held.at[i], read.at[i]) for i, source in enumerate(sources)
    ]
    width = held.shape[2] // parts
    sends = [
        pltpu.make_async_copy(held.at[:, :, pl.ds(i * width, width)], outs[i], sent.at[i])
        for i in range(parts)
    ]
    for copy in reads:
        copy.start()
    for copy in reads:
        copy.wait()
    for copy in sends:
        copy.start()
    for copy in sends:
        copy.wait()


def join(token, me, got, parts):
    cap, rows, aux = got[0].shape[-3:]
    n_occ = got[0].shape[0] if len(got) == 1 else len(got) + 1
    shape = jax.ShapeDtypeStruct((n_occ - 1, cap, rows // parts, aux), got[0].dtype)
    done = pl.pallas_call(
        functools.partial(join_kernel, n_occ, len(got), parts),
        out_shape=[jax.ShapeDtypeStruct(token.shape, token.dtype)] + [shape] * parts,
        in_specs=[SMEM] + [ANY] * (1 + len(got)),
        out_specs=[ANY] * (1 + parts),
        scratch_shapes=[
            pltpu.VMEM((n_occ - 1, cap, rows, aux), got[0].dtype),
            pltpu.SemaphoreType.DMA((n_occ,)),
            pltpu.SemaphoreType.DMA((parts,)),
        ],
        input_output_aliases={1: 0},
        compiler_params=pltpu.CompilerParams(vmem_limit_bytes=VMEM_LIMIT),
        cost_estimate=SMALL,
    )(me, token, *got)
    return done[0], done[1:]


def runs(flags, low, high):
    out = []
    for p in range(low, high):
        if out and flags[p] == out[-1][2]:
            out[-1] = (out[-1][0], p + 1, flags[p])
        else:
            out.append((p, p + 1, flags[p]))
    return out


def density_kernel(
    n_occ, n_blocks, cuts, jobs, held, last, me, sizes, order, eps_occ, va, vb, *refs
):
    refs = list(refs)
    refs.pop(0)
    n_parts = sum(cuts)
    first_blocks = [refs.pop(0) for _ in range(n_blocks)]
    units, chunks, row_chunks = plan(cuts, jobs)
    col_blocks = {c: [refs.pop(0) for _ in range(n_blocks)] for c in chunks}
    own = {c: col_blocks[c][0] if c in chunks else refs.pop(0) for c in row_chunks}
    before = refs.pop(0) if any(held) else None
    refs.pop(0)
    out, rows, cols, kbuf, abuf, total, result, sems = refs
    width, aux = rows.shape[2], rows.shape[3]
    part = width // n_parts
    n_copies = 0

    def copy(source, target):
        nonlocal n_copies
        made = pltpu.make_async_copy(source, target, sems.at[n_copies])
        made.start()
        n_copies += 1
        return made

    def load_rows(c):
        place = pl.ds(sum(cuts[:c]) * part, cuts[c] * part)
        return [
            copy(first_blocks[0].at[:, place], rows.at[0, :, place]),
            copy(own[c], rows.at[pl.ds(1, n_occ - 1), :, place]),
        ]

    def load_cols(unit, first, count):
        index, slots = units.index(unit), pl.ds(first, count)
        c = chunk_of(cuts, unit)
        inside = pl.ds((unit - sum(cuts[:c])) * part, part)
        copies = []
        for b in range(n_blocks):
            place = pl.ds(b * part, part)
            copies.append(
                copy(
                    first_blocks[b].at[slots, pl.ds(unit * part, part)],
                    cols.at[index, 0, slots, place],
                )
            )
            copies.append(
                copy(
                    col_blocks[c][b].at[:, slots, inside],
                    cols.at[index, pl.ds(1, n_occ - 1), slots, place],
                )
            )
        return copies

    def needed_rows(job):
        return [c for c in row_chunks if job[0] < sum(cuts[: c + 1]) and sum(cuts[:c]) < job[1]]

    row_copies = {c: load_rows(c) for c in needed_rows(jobs[0])}
    col_copies = {
        (units[0], first): load_cols(units[0], first, count)
        for first, count in ((0, 2), (2, 2), (4, 2))
    }
    for c in row_chunks:
        if c not in row_copies:
            row_copies[c] = load_rows(c)
    for unit in units[1:]:
        col_copies[unit, 0] = load_cols(unit, 0, CAP)
    total_copies = []
    energy = []
    for orbital, live in group_slots(sizes, order, me[0], n_occ):
        energy.append(jnp.where(live, eps_occ[orbital], jnp.float32(0.0)))

    def combine(low, n_rows, unit, at, i, j):
        step = 32 if n_rows % 32 == 0 else 16
        for r in range(0, n_rows, step):
            gap = (energy[i] + energy[j]) - (va[pl.ds(low + r, step), :] + vb[unit])
            inverse = pltpu.reciprocal(gap, approx=True)
            inverse = inverse * (2.0 - gap * inverse)
            upper = kbuf[j, pl.ds(i * n_rows + r, step), :]
            if i == j:
                abuf[pl.ds(i * n_rows + r, step), pl.ds(at + j * LANES, LANES)] = (
                    upper * inverse
                ).astype(abuf.dtype)
            else:
                lower = kbuf[i, pl.ds(j * n_rows + r, step), :]
                abuf[pl.ds(i * n_rows + r, step), pl.ds(at + j * LANES, LANES)] = (
                    (upper + upper - lower) * inverse
                ).astype(abuf.dtype)
                abuf[pl.ds(j * n_rows + r, step), pl.ds(at + i * LANES, LANES)] = (
                    (lower + lower - upper) * inverse
                ).astype(abuf.dtype)

    span = min(n_occ, max(1, 1024 // aux))
    spans = [(s, span) for s in range(0, n_occ - span, span)]
    tail = max(1, span // 2)
    spans += [(s, tail) for s in range(n_occ - span, n_occ, tail)]
    flags = list(held)
    sent = []
    for number, (low, high, chosen) in enumerate(jobs):
        first_row, n_rows = low * part, (high - low) * part
        for c in needed_rows((low, high)):
            for made in row_copies.pop(c, ()):
                made.wait()
        for slot, unit in enumerate(chosen):
            index = units.index(unit)
            for j in range(CAP + 1):
                for made in col_copies.pop((unit, j), ()):
                    made.wait()
                if number == 0 and slot == 0 and j == 2:
                    total_copies = [
                        copy(before.at[:, pl.ds(a * part, (b - a) * part)], total.at[:, pl.ds(a * part, (b - a) * part)])
                        for a, b, flag in runs(held, 0, n_parts)
                        if flag
                    ]
                if j < CAP:
                    left = jnp.concatenate(
                        [
                            rows[s, :, first_row : first_row + n_rows].reshape(CAP * n_rows, aux)
                            for s in range(n_occ)
                        ],
                        axis=1,
                    )
                    right = jnp.concatenate([cols[index, s, j] for s in range(n_occ)], axis=1)
                    kbuf[j, pl.ds(0, CAP * n_rows)] = lax.dot_general(
                        left, right, (((1,), (1,)), ((), ())), preferred_element_type=jnp.float32
                    )
                for i in range(j):
                    combine(first_row, n_rows, unit, slot * CAP * LANES, i, j - 1)
        if number == 0:
            for made in total_copies:
                made.wait()
        depth = len(chosen) * CAP * LANES
        for s, span in spans:
            lanes = pl.ds(s * aux, span * aux)
            right = jnp.concatenate(
                [
                    jnp.concatenate(
                        [cols[units.index(unit), t].reshape(CAP * LANES, aux) for unit in chosen],
                        axis=0,
                    )
                    for t in range(s, s + span)
                ],
                axis=1,
            )
            added = jnp.dot(
                abuf[pl.ds(0, CAP * n_rows), pl.ds(0, depth)], right, preferred_element_type=jnp.float32
            ).reshape(CAP, n_rows, span * aux)
            final = number == len(jobs) - 1
            for a, b, flag in runs(flags, low, high):
                where = pl.ds(a * part, (b - a) * part)
                piece = added[:, (a - low) * part : (b - low) * part]
                if flag:
                    piece = piece + total[:, where, lanes]
                if last and final:
                    result[:, where, lanes] = piece.astype(result.dtype)
                else:
                    total[:, where, lanes] = piece
            if final:
                if last:
                    for t in range(s, s + span):
                        place = pl.multiple_of((me[0] ^ t) * aux, aux)
                        sent.append(
                            copy(result.at[:, :, pl.ds(t * aux, aux)], out.at[:, :, pl.ds(place, aux)])
                        )
                else:
                    for a, b, flag in runs(
                        [f or low <= p < high for p, f in enumerate(flags)], 0, n_parts
                    ):
                        where = pl.ds(a * part, (b - a) * part)
                        if flag:
                            sent.append(
                                copy(total.at[:, where, lanes], out.at[:, where, lanes])
                            )
        flags = [f or low <= p < high for p, f in enumerate(flags)]
    for made in sent:
        made.wait()


def chunk_of(cuts, unit):
    return next(c for c in range(len(cuts)) if unit < sum(cuts[: c + 1]))


def plan(cuts, jobs):
    units = []
    for _, _, chosen in jobs:
        units += [unit for unit in chosen if unit not in units]
    chunks = sorted({chunk_of(cuts, unit) for unit in units})
    rows = sorted({chunk_of(cuts, p) for low, high, _ in jobs for p in range(low, high)})
    return units, chunks, rows


def density(token, scalars, first_blocks, blocks, before, held, jobs, last, cuts):
    n_blocks = len(first_blocks)
    width, aux = first_blocks[0].shape[1:]
    part = width // sum(cuts)
    n_occ = blocks[0][0].shape[0] + 1
    naux = n_occ * aux
    units, chunks, row_chunks = plan(cuts, jobs)
    kept = jnp.bfloat16 if last else jnp.float32
    deepest = max(len(chosen) for _, _, chosen in jobs)
    tallest = max(high - low for low, high, _ in jobs) * part * CAP
    operands = [*scalars, token, *first_blocks]
    for c in chunks:
        operands += blocks[c]
    operands += [blocks[c][0] for c in row_chunks if c not in chunks]
    operands += [before] if any(held) else []
    at = len(scalars)
    done = pl.pallas_call(
        functools.partial(density_kernel, n_occ, n_blocks, cuts, jobs, held, last),
        out_shape=[
            jax.ShapeDtypeStruct(token.shape, token.dtype),
            jax.ShapeDtypeStruct((CAP, width, naux), kept),
        ],
        in_specs=[SMEM] * 4 + [VMEM] * 2 + [ANY] * (len(operands) - at),
        out_specs=[ANY] * 2,
        scratch_shapes=[
            pltpu.VMEM((n_occ, CAP, width, aux), jnp.bfloat16),
            pltpu.VMEM((len(units), n_occ, CAP, LANES, aux), jnp.bfloat16),
            pltpu.VMEM((CAP, tallest, LANES), jnp.float32),
            pltpu.VMEM((tallest, deepest * CAP * LANES), jnp.bfloat16),
            pltpu.VMEM((CAP, width, naux), jnp.float32),
            pltpu.VMEM((CAP, width, naux) if last else (1, 16, 128), jnp.bfloat16),
            pltpu.SemaphoreType.DMA((48 + 2 * n_blocks * (len(units) + 4),)),
        ],
        input_output_aliases={at: 0},
        compiler_params=pltpu.CompilerParams(vmem_limit_bytes=VMEM_LIMIT),
        cost_estimate=SMALL,
    )(*operands)
    held = tuple(
        f or any(low <= p < high for low, high, _ in jobs) for p, f in enumerate(held)
    )
    return done[0], done[1], held


def on_device(basis, group_sizes, orbital_order, eps_occ, eps_vir):
    n_virt, n_occ = lax.axis_size("virt"), lax.axis_size("occ")
    me_occ, me_virt = lax.axis_index("occ"), lax.axis_index("virt")
    width, aux = basis.shape[1:]
    dims = (n_virt // 2).bit_length() - 1
    part = LANES // n_virt
    n_parts = width // part
    me = me_occ.reshape(1).astype(jnp.int32)
    n_own = 1 << dims

    def bit(dim, core):
        return 2 << ((dim + core) % dims)

    def hop(block, dim):
        pairs = [(d, d ^ bit(dim, d & 1)) for d in range(n_virt)]
        return lax.ppermute(block, "virt", pairs)

    def sibling(block):
        return lax.ppermute(block, "virt", [(d, d ^ 1) for d in range(n_virt)])

    def across(block, mask):
        return lax.ppermute(block, "occ", [(d, d ^ mask) for d in range(n_occ)])

    def origin(mask, core):
        return sum(bit(dim, core) for dim in range(dims) if mask >> dim & 1)

    core = me_virt & 1
    origins = [
        me_virt ^ jnp.where(core == 0, origin(m, 0), origin(m, 1)) for m in range(n_own)
    ] + [
        me_virt ^ 1 ^ jnp.where(core == 0, origin(m, 1), origin(m, 0)) for m in range(n_own)
    ]
    by_owner = eps_vir.reshape(n_virt, n_parts, part)
    vb = by_owner[jnp.stack(origins)].transpose(1, 0, 2).reshape(n_parts, 1, LANES)
    va = lax.dynamic_slice_in_dim(eps_vir, me_virt * width, width).reshape(width, 1)
    scalars = (me, group_sizes, orbital_order, eps_occ, va, vb)

    z_parts = (1, 2, 2)
    cuts = z_parts
    starts = [sum(cuts[:c]) * part for c in range(len(cuts) + 1)]
    sends = []
    token = jnp.zeros((8, 128), jnp.float32)
    token, send, first = stage(token, basis, *scalars[:3], n_occ, 0, starts[1], with_own=True)
    sends.append([send])
    blocks = {}

    def spread(name, block):
        held = blocks[name] = [block] + [None] * (2 * n_own - 1)
        held[n_own] = sibling(block)
        for dim in range(dims):
            held[1 << dim] = hop(block, dim)

    def relay(token, name, level):
        held = blocks[name]
        arrived = [m for m in range(1, n_own) if m.bit_count() == level]
        token, gated = gate(token, (), [held[m] for m in arrived])
        for m, block in zip(arrived, gated):
            held[m] = block
        for m in arrived:
            for dim in range(m.bit_length(), dims):
                held[m | 1 << dim] = hop(held[m], dim)
        for m in arrived:
            held[n_own + m] = sibling(held[m])
        return token

    crossing = []
    n_chunks = len(z_parts)

    def cross(token, c):
        token, gated = gate(token, (), sends[c])
        if len(gated) == 1:
            crossing.append([lax.all_to_all(gated[0], "occ", 0, 0, tiled=True)])
        else:
            crossing.append([across(block, mask) for mask, block in enumerate(gated, 1)])
        return token

    total, held = None, (False,) * n_parts

    def add(jobs, last=False):
        nonlocal token, total, held
        token, total, held = density(
            token, scalars, blocks["first"], chunks, total, held, jobs, last, cuts
        )

    def arrive(name):
        nonlocal token
        for level in range(2, dims + 1):
            token = relay(token, name, level)

    chunks = {}

    def collect(c):
        nonlocal token
        token, (block,) = join(token, me, crossing[c], 1)
        spread(c, block)
        chunks[c] = blocks[c]

    token = cross(token, 0)
    spread("first", first)
    for c in range(1, n_chunks):
        token, *send = stage(token, basis, *scalars[:3], n_occ, starts[c], starts[c + 1])
        sends.append(send)
    for c in range(1, n_chunks):
        token = cross(token, c)
    collect(0)
    token = relay(token, "first", 1)
    arrive("first")
    token = relay(token, 0, 1)
    arrive(0)
    collect(1)
    early = cuts[0] + cuts[1]
    add([(0, early, (0,))])
    token = relay(token, 1, 1)
    collect(2)
    arrive(1)
    add([(early, n_parts, (0,)), (0, n_parts, (1,))])
    token = relay(token, 2, 1)
    add([(0, n_parts, (2,))])
    arrive(2)
    add([(0, n_parts, (3, 4))], True)
    return total.reshape(1, CAP, width, n_occ * aux)


def solution(mesh):
    return jax.shard_map(
        on_device,
        mesh=mesh,
        in_specs=(P(None, "virt", "occ"), P(), P(), P(), P()),
        out_specs=P("occ", None, "virt", None),
        check_vma=False,
    )
```

```python
import functools

import jax
import jax.numpy as jnp
from jax import lax
from jax.experimental import pallas as pl
from jax.experimental.pallas import tpu as pltpu
from jax.sharding import PartitionSpec as P

CAP = 6
LANES = 256
VMEM_LIMIT = (64 << 20) - (512 << 10)
SMALL = pl.CostEstimate(flops=1 << 10, bytes_accessed=1 << 10, transcendentals=0)
ANY = pl.BlockSpec(memory_space=pl.ANY)
VMEM = pl.BlockSpec(memory_space=pltpu.VMEM)
SMEM = pl.BlockSpec(memory_space=pltpu.SMEM)


def group_slots(sizes, order, group, n_groups):
    offset = jnp.int32(0)
    count = jnp.int32(0)
    for other in range(n_groups):
        offset = offset + jnp.where(other < group, sizes[other], 0)
        count = count + jnp.where(other == group, sizes[other], 0)
    last = order.shape[0] - 1
    return [
        (order[jnp.minimum(offset + slot, last)], slot < count) for slot in range(CAP)
    ]


def stage_kernel(n_occ, low, high, with_own, split, me, sizes, order, basis, *refs):
    refs = refs if with_own else refs[1:]
    outs, own, (held, read, sent) = refs[1:-3], refs[-4], refs[-3:]
    if with_own:
        refs[0][...] = jnp.zeros(refs[0].shape, refs[0].dtype)
    reads = []
    copies = []
    rows = pl.ds(low, high - low)
    for mask in range(n_occ):
        whole = with_own and mask == 0
        for slot, (orbital, live) in enumerate(
            group_slots(sizes, order, me[0] ^ mask, n_occ)
        ):
            index = mask * CAP + slot
            if whole:
                copy = pltpu.make_async_copy(basis.at[orbital], held.at[0, slot], read.at[index])
            else:
                copy = pltpu.make_async_copy(
                    basis.at[orbital, rows], held.at[mask, slot, pl.ds(0, high - low)], read.at[index]
                )
            copy.start()
            reads.append((copy, live))
    for mask in range(n_occ):
        for slot in range(CAP):
            copy, live = reads[mask * CAP + slot]
            copy.wait()

            @pl.when(jnp.logical_not(live))
            def _():
                held[mask, slot] = jnp.zeros(held.shape[2:], held.dtype)

        if mask or not split:
            target = outs[mask - 1] if split else outs[0].at[me[0] ^ mask]
            copies.append(
                pltpu.make_async_copy(held.at[mask, :, pl.ds(0, high - low)], target, sent.at[mask])
            )
            copies[-1].start()
        if with_own and mask == 0:
            copies.append(pltpu.make_async_copy(held.at[0], own, sent.at[n_occ]))
            copies[-1].start()
    for copy in copies:
        copy.wait()


def stage(token, basis, me, sizes, order, n_occ, low, high, with_own=False, split=False):
    width, aux = basis.shape[1:]
    piece = (CAP, high - low, aux)
    shapes = [piece] * (n_occ - 1) if split else [(n_occ, *piece)]
    shapes += [(CAP, width, aux)] * with_own
    return pl.pallas_call(
        functools.partial(stage_kernel, n_occ, low, high, with_own, split),
        out_shape=[
            jax.ShapeDtypeStruct((8, 128), jnp.float32),
            *[jax.ShapeDtypeStruct(shape, basis.dtype) for shape in shapes],
        ],
        in_specs=[SMEM, SMEM, SMEM, ANY] + [ANY] * (not with_own),
        out_specs=[VMEM if with_own else ANY] + [ANY] * len(shapes),
        scratch_shapes=[
            pltpu.VMEM((n_occ, CAP, width if with_own else high - low, aux), basis.dtype),
            pltpu.SemaphoreType.DMA((n_occ * CAP,)),
            pltpu.SemaphoreType.DMA((1 + n_occ,)),
        ],
        input_output_aliases={} if with_own else {4: 0},
        compiler_params=pltpu.CompilerParams(vmem_limit_bytes=VMEM_LIMIT),
        cost_estimate=SMALL,
    )(me, sizes, order, basis, *([] if with_own else [token]))


def gate(token, needs=(), gives=()):
    operands = [token, *gives, *needs]
    kept = 1 + len(gives)
    done = pl.pallas_call(
        lambda *refs: None,
        out_shape=[jax.ShapeDtypeStruct(x.shape, x.dtype) for x in operands[:kept]],
        in_specs=[ANY] * len(operands),
        out_specs=[ANY] * kept,
        input_output_aliases={i: i for i in range(kept)},
        compiler_params=pltpu.CompilerParams(vmem_limit_bytes=VMEM_LIMIT),
        cost_estimate=SMALL,
    )(*operands)
    return done[0], done[1:]


def join_kernel(n_occ, n_got, parts, me, token_in, *refs):
    got, outs, (held, read, sent) = refs[:n_got], refs[n_got + 1 : -3], refs[-3:]
    sources = got if n_got > 1 else [got[0].at[me[0] ^ mask] for mask in range(1, n_occ)]
    reads = [
        pltpu.make_async_copy(source, held.at[i], read.at[i]) for i, source in enumerate(sources)
    ]
    width = held.shape[2] // parts
    sends = [
        pltpu.make_async_copy(held.at[:, :, pl.ds(i * width, width)], outs[i], sent.at[i])
        for i in range(parts)
    ]
    for copy in reads:
        copy.start()
    for copy in reads:
        copy.wait()
    for copy in sends:
        copy.start()
    for copy in sends:
        copy.wait()


def join(token, me, got, parts):
    cap, rows, aux = got[0].shape[-3:]
    n_occ = got[0].shape[0] if len(got) == 1 else len(got) + 1
    shape = jax.ShapeDtypeStruct((n_occ - 1, cap, rows // parts, aux), got[0].dtype)
    done = pl.pallas_call(
        functools.partial(join_kernel, n_occ, len(got), parts),
        out_shape=[jax.ShapeDtypeStruct(token.shape, token.dtype)] + [shape] * parts,
        in_specs=[SMEM] + [ANY] * (1 + len(got)),
        out_specs=[ANY] * (1 + parts),
        scratch_shapes=[
            pltpu.VMEM((n_occ - 1, cap, rows, aux), got[0].dtype),
            pltpu.SemaphoreType.DMA((n_occ,)),
            pltpu.SemaphoreType.DMA((parts,)),
        ],
        input_output_aliases={1: 0},
        compiler_params=pltpu.CompilerParams(vmem_limit_bytes=VMEM_LIMIT),
        cost_estimate=SMALL,
    )(me, token, *got)
    return done[0], done[1:]


def runs(flags, low, high):
    out = []
    for p in range(low, high):
        if out and flags[p] == out[-1][2]:
            out[-1] = (out[-1][0], p + 1, flags[p])
        else:
            out.append((p, p + 1, flags[p]))
    return out


def density_kernel(
    n_occ, n_blocks, cuts, jobs, held, last, me, sizes, order, eps_occ, va, vb, *refs
):
    refs = list(refs)
    refs.pop(0)
    n_parts = sum(cuts)
    first_blocks = [refs.pop(0) for _ in range(n_blocks)]
    units, chunks, row_chunks = plan(cuts, jobs)
    col_blocks = {c: [refs.pop(0) for _ in range(n_blocks)] for c in chunks}
    own = {c: col_blocks[c][0] if c in chunks else refs.pop(0) for c in row_chunks}
    before = refs.pop(0) if any(held) else None
    refs.pop(0)
    out, rows, cols, kbuf, abuf, total, result, sems = refs
    width, aux = rows.shape[2], rows.shape[3]
    part = width // n_parts
    n_copies = 0

    def copy(source, target):
        nonlocal n_copies
        made = pltpu.make_async_copy(source, target, sems.at[n_copies])
        made.start()
        n_copies += 1
        return made

    def load_rows(c):
        place = pl.ds(sum(cuts[:c]) * part, cuts[c] * part)
        return [
            copy(first_blocks[0].at[:, place], rows.at[0, :, place]),
            copy(own[c], rows.at[pl.ds(1, n_occ - 1), :, place]),
        ]

    def load_cols(unit, first, count):
        index, slots = units.index(unit), pl.ds(first, count)
        c = chunk_of(cuts, unit)
        inside = pl.ds((unit - sum(cuts[:c])) * part, part)
        copies = []
        for b in range(n_blocks):
            place = pl.ds(b * part, part)
            copies.append(
                copy(
                    first_blocks[b].at[slots, pl.ds(unit * part, part)],
                    cols.at[index, 0, slots, place],
                )
            )
            copies.append(
                copy(
                    col_blocks[c][b].at[:, slots, inside],
                    cols.at[index, pl.ds(1, n_occ - 1), slots, place],
                )
            )
        return copies

    def needed_rows(job):
        return [c for c in row_chunks if job[0] < sum(cuts[: c + 1]) and sum(cuts[:c]) < job[1]]

    row_copies = {c: load_rows(c) for c in needed_rows(jobs[0])}
    col_copies = {
        (units[0], first): load_cols(units[0], first, count)
        for first, count in ((0, 2), (2, 2), (4, 2))
    }
    for c in row_chunks:
        if c not in row_copies:
            row_copies[c] = load_rows(c)
    for unit in units[1:]:
        col_copies[unit, 0] = load_cols(unit, 0, CAP)
    total_copies = []
    energy = []
    for orbital, live in group_slots(sizes, order, me[0], n_occ):
        energy.append(jnp.where(live, eps_occ[orbital], jnp.float32(0.0)))

    def combine(low, n_rows, unit, at, i, j):
        step = 32 if n_rows % 32 == 0 else 16
        for r in range(0, n_rows, step):
            gap = (energy[i] + energy[j]) - (va[pl.ds(low + r, step), :] + vb[unit])
            inverse = pltpu.reciprocal(gap, approx=True)
            inverse = inverse * (2.0 - gap * inverse)
            upper = kbuf[j, pl.ds(i * n_rows + r, step), :]
            if i == j:
                abuf[pl.ds(i * n_rows + r, step), pl.ds(at + j * LANES, LANES)] = (
                    upper * inverse
                ).astype(abuf.dtype)
            else:
                lower = kbuf[i, pl.ds(j * n_rows + r, step), :]
                abuf[pl.ds(i * n_rows + r, step), pl.ds(at + j * LANES, LANES)] = (
                    (upper + upper - lower) * inverse
                ).astype(abuf.dtype)
                abuf[pl.ds(j * n_rows + r, step), pl.ds(at + i * LANES, LANES)] = (
                    (lower + lower - upper) * inverse
                ).astype(abuf.dtype)

    span = min(n_occ, max(1, 1024 // aux))
    spans = [(s, span) for s in range(0, n_occ - span, span)]
    tail = max(1, span // 2)
    spans += [(s, tail) for s in range(n_occ - span, n_occ, tail)]
    flags = list(held)
    sent = []
    for number, (low, high, chosen) in enumerate(jobs):
        first_row, n_rows = low * part, (high - low) * part
        for c in needed_rows((low, high)):
            for made in row_copies.pop(c, ()):
                made.wait()
        for slot, unit in enumerate(chosen):
            index = units.index(unit)
            for j in range(CAP + 1):
                for made in col_copies.pop((unit, j), ()):
                    made.wait()
                if number == 0 and slot == 0 and j == 2:
                    total_copies = [
                        copy(before.at[:, pl.ds(a * part, (b - a) * part)], total.at[:, pl.ds(a * part, (b - a) * part)])
                        for a, b, flag in runs(held, 0, n_parts)
                        if flag
                    ]
                if j < CAP:
                    left = jnp.concatenate(
                        [
                            rows[s, :, first_row : first_row + n_rows].reshape(CAP * n_rows, aux)
                            for s in range(n_occ)
                        ],
                        axis=1,
                    )
                    right = jnp.concatenate([cols[index, s, j] for s in range(n_occ)], axis=1)
                    kbuf[j, pl.ds(0, CAP * n_rows)] = lax.dot_general(
                        left, right, (((1,), (1,)), ((), ())), preferred_element_type=jnp.float32
                    )
                for i in range(j):
                    combine(first_row, n_rows, unit, slot * CAP * LANES, i, j - 1)
        if number == 0:
            for made in total_copies:
                made.wait()
        depth = len(chosen) * CAP * LANES
        for s, span in spans:
            lanes = pl.ds(s * aux, span * aux)
            right = jnp.concatenate(
                [
                    jnp.concatenate(
                        [cols[units.index(unit), t].reshape(CAP * LANES, aux) for unit in chosen],
                        axis=0,
                    )
                    for t in range(s, s + span)
                ],
                axis=1,
            )
            added = jnp.dot(
                abuf[pl.ds(0, CAP * n_rows), pl.ds(0, depth)], right, preferred_element_type=jnp.float32
            ).reshape(CAP, n_rows, span * aux)
            final = number == len(jobs) - 1
            for a, b, flag in runs(flags, low, high):
                where = pl.ds(a * part, (b - a) * part)
                piece = added[:, (a - low) * part : (b - low) * part]
                if flag:
                    piece = piece + total[:, where, lanes]
                if last and final:
                    result[:, where, lanes] = piece.astype(result.dtype)
                else:
                    total[:, where, lanes] = piece
            if final:
                if last:
                    for t in range(s, s + span):
                        place = pl.multiple_of((me[0] ^ t) * aux, aux)
                        sent.append(
                            copy(result.at[:, :, pl.ds(t * aux, aux)], out.at[:, :, pl.ds(place, aux)])
                        )
                else:
                    for a, b, flag in runs(
                        [f or low <= p < high for p, f in enumerate(flags)], 0, n_parts
                    ):
                        where = pl.ds(a * part, (b - a) * part)
                        if flag:
                            sent.append(
                                copy(total.at[:, where, lanes], out.at[:, where, lanes])
                            )
        flags = [f or low <= p < high for p, f in enumerate(flags)]
    for made in sent:
        made.wait()


def chunk_of(cuts, unit):
    return next(c for c in range(len(cuts)) if unit < sum(cuts[: c + 1]))


def plan(cuts, jobs):
    units = []
    for _, _, chosen in jobs:
        units += [unit for unit in chosen if unit not in units]
    chunks = sorted({chunk_of(cuts, unit) for unit in units})
    rows = sorted({chunk_of(cuts, p) for low, high, _ in jobs for p in range(low, high)})
    return units, chunks, rows


def density(token, scalars, first_blocks, blocks, before, held, jobs, last, cuts):
    n_blocks = len(first_blocks)
    width, aux = first_blocks[0].shape[1:]
    part = width // sum(cuts)
    n_occ = blocks[0][0].shape[0] + 1
    naux = n_occ * aux
    units, chunks, row_chunks = plan(cuts, jobs)
    kept = jnp.bfloat16 if last else jnp.float32
    deepest = max(len(chosen) for _, _, chosen in jobs)
    tallest = max(high - low for low, high, _ in jobs) * part * CAP
    operands = [*scalars, token, *first_blocks]
    for c in chunks:
        operands += blocks[c]
    operands += [blocks[c][0] for c in row_chunks if c not in chunks]
    operands += [before] if any(held) else []
    at = len(scalars)
    done = pl.pallas_call(
        functools.partial(density_kernel, n_occ, n_blocks, cuts, jobs, held, last),
        out_shape=[
            jax.ShapeDtypeStruct(token.shape, token.dtype),
            jax.ShapeDtypeStruct((CAP, width, naux), kept),
        ],
        in_specs=[SMEM] * 4 + [VMEM] * 2 + [ANY] * (len(operands) - at),
        out_specs=[ANY] * 2,
        scratch_shapes=[
            pltpu.VMEM((n_occ, CAP, width, aux), jnp.bfloat16),
            pltpu.VMEM((len(units), n_occ, CAP, LANES, aux), jnp.bfloat16),
            pltpu.VMEM((CAP, tallest, LANES), jnp.float32),
            pltpu.VMEM((tallest, deepest * CAP * LANES), jnp.bfloat16),
            pltpu.VMEM((CAP, width, naux), jnp.float32),
            pltpu.VMEM((CAP, width, naux) if last else (1, 16, 128), jnp.bfloat16),
            pltpu.SemaphoreType.DMA((48 + 2 * n_blocks * (len(units) + 4),)),
        ],
        input_output_aliases={at: 0},
        compiler_params=pltpu.CompilerParams(vmem_limit_bytes=VMEM_LIMIT),
        cost_estimate=SMALL,
    )(*operands)
    held = tuple(
        f or any(low <= p < high for low, high, _ in jobs) for p, f in enumerate(held)
    )
    return done[0], done[1], held


def on_device(basis, group_sizes, orbital_order, eps_occ, eps_vir):
    n_virt, n_occ = lax.axis_size("virt"), lax.axis_size("occ")
    me_occ, me_virt = lax.axis_index("occ"), lax.axis_index("virt")
    width, aux = basis.shape[1:]
    dims = (n_virt // 2).bit_length() - 1
    part = LANES // n_virt
    n_parts = width // part
    me = me_occ.reshape(1).astype(jnp.int32)
    n_own = 1 << dims

    def bit(dim, core):
        return 2 << ((dim + core) % dims)

    def hop(block, dim):
        pairs = [(d, d ^ bit(dim, d & 1)) for d in range(n_virt)]
        return lax.ppermute(block, "virt", pairs)

    def sibling(block):
        return lax.ppermute(block, "virt", [(d, d ^ 1) for d in range(n_virt)])

    def across(block, mask):
        return lax.ppermute(block, "occ", [(d, d ^ mask) for d in range(n_occ)])

    def origin(mask, core):
        return sum(bit(dim, core) for dim in range(dims) if mask >> dim & 1)

    core = me_virt & 1
    origins = [
        me_virt ^ jnp.where(core == 0, origin(m, 0), origin(m, 1)) for m in range(n_own)
    ] + [
        me_virt ^ 1 ^ jnp.where(core == 0, origin(m, 1), origin(m, 0)) for m in range(n_own)
    ]
    by_owner = eps_vir.reshape(n_virt, n_parts, part)
    vb = by_owner[jnp.stack(origins)].transpose(1, 0, 2).reshape(n_parts, 1, LANES)
    va = lax.dynamic_slice_in_dim(eps_vir, me_virt * width, width).reshape(width, 1)
    scalars = (me, group_sizes, orbital_order, eps_occ, va, vb)

    z_parts = (1, 2, 2)
    cuts = z_parts
    starts = [sum(cuts[:c]) * part for c in range(len(cuts) + 1)]
    sends = []
    token, send, first = stage(None, basis, *scalars[:3], n_occ, 0, starts[1], with_own=True)
    sends.append([send])
    blocks = {}

    def spread(name, block):
        held = blocks[name] = [block] + [None] * (2 * n_own - 1)
        held[n_own] = sibling(block)
        for dim in range(dims):
            held[1 << dim] = hop(block, dim)

    def relay(token, name, level):
        held = blocks[name]
        arrived = [m for m in range(1, n_own) if m.bit_count() == level]
        token, gated = gate(token, (), [held[m] for m in arrived])
        for m, block in zip(arrived, gated):
            held[m] = block
        for m in arrived:
            for dim in range(m.bit_length(), dims):
                held[m | 1 << dim] = hop(held[m], dim)
        for m in arrived:
            held[n_own + m] = sibling(held[m])
        return token

    crossing = []
    n_chunks = len(z_parts)

    def cross(token, c):
        token, gated = gate(token, (), sends[c])
        if len(gated) == 1:
            crossing.append([lax.all_to_all(gated[0], "occ", 0, 0, tiled=True)])
        else:
            crossing.append([across(block, mask) for mask, block in enumerate(gated, 1)])
        return token

    total, held = None, (False,) * n_parts

    def add(jobs, last=False):
        nonlocal token, total, held
        token, total, held = density(
            token, scalars, blocks["first"], chunks, total, held, jobs, last, cuts
        )

    def arrive(name):
        nonlocal token
        for level in range(2, dims + 1):
            token = relay(token, name, level)

    chunks = {}

    def collect(c):
        nonlocal token
        token, (block,) = join(token, me, crossing[c], 1)
        spread(c, block)
        chunks[c] = blocks[c]

    token = cross(token, 0)
    spread("first", first)
    for c in range(1, n_chunks):
        token, *send = stage(token, basis, *scalars[:3], n_occ, starts[c], starts[c + 1])
        sends.append(send)
    for c in range(1, n_chunks):
        token = cross(token, c)
    token, _ = gate(token, (va, vb))
    collect(0)
    token = relay(token, "first", 1)
    arrive("first")
    token = relay(token, 0, 1)
    collect(1)
    arrive(0)
    early = cuts[0] + cuts[1]
    add([(0, early, (0,))])
    token = relay(token, 1, 1)
    collect(2)
    arrive(1)
    add([(early, n_parts, (0,)), (0, n_parts, (1,))])
    token = relay(token, 2, 1)
    add([(0, n_parts, (2,))])
    arrive(2)
    add([(0, n_parts, (3, 4))], True)
    return total.reshape(1, CAP, width, n_occ * aux)


def solution(mesh):
    return jax.shard_map(
        on_device,
        mesh=mesh,
        in_specs=(P(None, "virt", "occ"), P(), P(), P(), P()),
        out_specs=P("occ", None, "virt", None),
        check_vma=False,
    )
```

```python
import functools

import jax
import jax.numpy as jnp
from jax import lax
from jax.experimental import pallas as pl
from jax.experimental.pallas import tpu as pltpu
from jax.sharding import PartitionSpec as P

CAP = 6
LANES = 256
VMEM_LIMIT = (64 << 20) - (512 << 10)
SMALL = pl.CostEstimate(flops=1 << 10, bytes_accessed=1 << 10, transcendentals=0)
ANY = pl.BlockSpec(memory_space=pl.ANY)
VMEM = pl.BlockSpec(memory_space=pltpu.VMEM)
SMEM = pl.BlockSpec(memory_space=pltpu.SMEM)


def group_slots(sizes, order, group, n_groups):
    offset = jnp.int32(0)
    count = jnp.int32(0)
    for other in range(n_groups):
        offset = offset + jnp.where(other < group, sizes[other], 0)
        count = count + jnp.where(other == group, sizes[other], 0)
    last = order.shape[0] - 1
    return [
        (order[jnp.minimum(offset + slot, last)], slot < count) for slot in range(CAP)
    ]


def stage_kernel(n_occ, low, high, with_own, split, me, sizes, order, basis, *refs):
    refs = refs if with_own else refs[1:]
    outs, own, (held, read, sent) = refs[1:-3], refs[-4], refs[-3:]
    if with_own:
        refs[0][...] = jnp.zeros(refs[0].shape, refs[0].dtype)
    reads = []
    copies = []
    rows = pl.ds(low, high - low)
    for mask in range(n_occ):
        whole = with_own and mask == 0
        for slot, (orbital, live) in enumerate(
            group_slots(sizes, order, me[0] ^ mask, n_occ)
        ):
            index = mask * CAP + slot
            if whole:
                copy = pltpu.make_async_copy(basis.at[orbital], held.at[0, slot], read.at[index])
            else:
                copy = pltpu.make_async_copy(
                    basis.at[orbital, rows], held.at[mask, slot, pl.ds(0, high - low)], read.at[index]
                )
            copy.start()
            reads.append((copy, live))
    for mask in range(n_occ):
        for slot in range(CAP):
            copy, live = reads[mask * CAP + slot]
            copy.wait()

            @pl.when(jnp.logical_not(live))
            def _():
                held[mask, slot] = jnp.zeros(held.shape[2:], held.dtype)

        if mask or not split:
            target = outs[mask - 1] if split else outs[0].at[me[0] ^ mask]
            copies.append(
                pltpu.make_async_copy(held.at[mask, :, pl.ds(0, high - low)], target, sent.at[mask])
            )
            copies[-1].start()
        if with_own and mask == 0:
            copies.append(pltpu.make_async_copy(held.at[0], own, sent.at[n_occ]))
            copies[-1].start()
    for copy in copies:
        copy.wait()


def stage(token, basis, me, sizes, order, n_occ, low, high, with_own=False, split=False):
    width, aux = basis.shape[1:]
    piece = (CAP, high - low, aux)
    shapes = [piece] * (n_occ - 1) if split else [(n_occ, *piece)]
    shapes += [(CAP, width, aux)] * with_own
    return pl.pallas_call(
        functools.partial(stage_kernel, n_occ, low, high, with_own, split),
        out_shape=[
            jax.ShapeDtypeStruct((8, 128), jnp.float32),
            *[jax.ShapeDtypeStruct(shape, basis.dtype) for shape in shapes],
        ],
        in_specs=[SMEM, SMEM, SMEM, ANY] + [ANY] * (not with_own),
        out_specs=[VMEM if with_own else ANY] + [ANY] * len(shapes),
        scratch_shapes=[
            pltpu.VMEM((n_occ, CAP, width if with_own else high - low, aux), basis.dtype),
            pltpu.SemaphoreType.DMA((n_occ * CAP,)),
            pltpu.SemaphoreType.DMA((1 + n_occ,)),
        ],
        input_output_aliases={} if with_own else {4: 0},
        compiler_params=pltpu.CompilerParams(vmem_limit_bytes=VMEM_LIMIT),
        cost_estimate=SMALL,
    )(me, sizes, order, basis, *([] if with_own else [token]))


def gate(token, needs=(), gives=()):
    operands = [token, *gives, *needs]
    kept = 1 + len(gives)
    done = pl.pallas_call(
        lambda *refs: None,
        out_shape=[jax.ShapeDtypeStruct(x.shape, x.dtype) for x in operands[:kept]],
        in_specs=[ANY] * len(operands),
        out_specs=[ANY] * kept,
        input_output_aliases={i: i for i in range(kept)},
        compiler_params=pltpu.CompilerParams(vmem_limit_bytes=VMEM_LIMIT),
        cost_estimate=SMALL,
    )(*operands)
    return done[0], done[1:]


def join_kernel(n_occ, n_got, parts, me, token_in, *refs):
    got, outs, (held, read, sent) = refs[:n_got], refs[n_got + 1 : -3], refs[-3:]
    sources = got if n_got > 1 else [got[0].at[me[0] ^ mask] for mask in range(1, n_occ)]
    reads = [
        pltpu.make_async_copy(source, held.at[i], read.at[i]) for i, source in enumerate(sources)
    ]
    width = held.shape[2] // parts
    sends = [
        pltpu.make_async_copy(held.at[:, :, pl.ds(i * width, width)], outs[i], sent.at[i])
        for i in range(parts)
    ]
    for copy in reads:
        copy.start()
    for copy in reads:
        copy.wait()
    for copy in sends:
        copy.start()
    for copy in sends:
        copy.wait()


def join(token, me, got, parts):
    cap, rows, aux = got[0].shape[-3:]
    n_occ = got[0].shape[0] if len(got) == 1 else len(got) + 1
    shape = jax.ShapeDtypeStruct((n_occ - 1, cap, rows // parts, aux), got[0].dtype)
    done = pl.pallas_call(
        functools.partial(join_kernel, n_occ, len(got), parts),
        out_shape=[jax.ShapeDtypeStruct(token.shape, token.dtype)] + [shape] * parts,
        in_specs=[SMEM] + [ANY] * (1 + len(got)),
        out_specs=[ANY] * (1 + parts),
        scratch_shapes=[
            pltpu.VMEM((n_occ - 1, cap, rows, aux), got[0].dtype),
            pltpu.SemaphoreType.DMA((n_occ,)),
            pltpu.SemaphoreType.DMA((parts,)),
        ],
        input_output_aliases={1: 0},
        compiler_params=pltpu.CompilerParams(vmem_limit_bytes=VMEM_LIMIT),
        cost_estimate=SMALL,
    )(me, token, *got)
    return done[0], done[1:]


def runs(flags, low, high):
    out = []
    for p in range(low, high):
        if out and flags[p] == out[-1][2]:
            out[-1] = (out[-1][0], p + 1, flags[p])
        else:
            out.append((p, p + 1, flags[p]))
    return out


def density_kernel(
    n_occ, n_blocks, cuts, jobs, held, last, *refs
):
    refs = list(refs)
    small = [refs.pop(0) for _ in range(6)]
    refs.pop(0)
    n_parts = sum(cuts)
    first_blocks = [refs.pop(0) for _ in range(n_blocks)]
    units, chunks, row_chunks = plan(cuts, jobs)
    col_blocks = {c: [refs.pop(0) for _ in range(n_blocks)] for c in chunks}
    own = {c: col_blocks[c][0] if c in chunks else refs.pop(0) for c in row_chunks}
    before = refs.pop(0) if any(held) else None
    refs.pop(0)
    out, me, sizes, order, eps_occ, va, vb, rows, cols, kbuf, abuf, total, result, sems = refs
    width, aux = rows.shape[2], rows.shape[3]
    part = width // n_parts
    n_copies = 0

    def copy(source, target):
        nonlocal n_copies
        made = pltpu.make_async_copy(source, target, sems.at[n_copies])
        made.start()
        n_copies += 1
        return made

    small_copies = [copy(a, b) for a, b in zip(small, (me, sizes, order, eps_occ, va, vb))]

    def load_rows(c):
        place = pl.ds(sum(cuts[:c]) * part, cuts[c] * part)
        return [
            copy(first_blocks[0].at[:, place], rows.at[0, :, place]),
            copy(own[c], rows.at[pl.ds(1, n_occ - 1), :, place]),
        ]

    def load_cols(unit, first, count):
        index, slots = units.index(unit), pl.ds(first, count)
        c = chunk_of(cuts, unit)
        inside = pl.ds((unit - sum(cuts[:c])) * part, part)
        copies = []
        for b in range(n_blocks):
            place = pl.ds(b * part, part)
            copies.append(
                copy(
                    first_blocks[b].at[slots, pl.ds(unit * part, part)],
                    cols.at[index, 0, slots, place],
                )
            )
            copies.append(
                copy(
                    col_blocks[c][b].at[:, slots, inside],
                    cols.at[index, pl.ds(1, n_occ - 1), slots, place],
                )
            )
        return copies

    def needed_rows(job):
        return [c for c in row_chunks if job[0] < sum(cuts[: c + 1]) and sum(cuts[:c]) < job[1]]

    row_copies = {c: load_rows(c) for c in needed_rows(jobs[0])}
    col_copies = {
        (units[0], first): load_cols(units[0], first, count)
        for first, count in ((0, 2), (2, 2), (4, 2))
    }
    for c in row_chunks:
        if c not in row_copies:
            row_copies[c] = load_rows(c)
    for unit in units[1:]:
        col_copies[unit, 0] = load_cols(unit, 0, CAP)
    total_copies = []
    for made in small_copies:
        made.wait()
    energy = []
    for orbital, live in group_slots(sizes, order, me[0], n_occ):
        energy.append(jnp.where(live, eps_occ[orbital], jnp.float32(0.0)))

    def combine(low, n_rows, unit, at, i, j):
        step = 32 if n_rows % 32 == 0 else 16
        for r in range(0, n_rows, step):
            gap = (energy[i] + energy[j]) - (va[pl.ds(low + r, step), :] + vb[unit])
            inverse = pltpu.reciprocal(gap, approx=True)
            inverse = inverse * (2.0 - gap * inverse)
            upper = kbuf[j, pl.ds(i * n_rows + r, step), :]
            if i == j:
                abuf[pl.ds(i * n_rows + r, step), pl.ds(at + j * LANES, LANES)] = (
                    upper * inverse
                ).astype(abuf.dtype)
            else:
                lower = kbuf[i, pl.ds(j * n_rows + r, step), :]
                abuf[pl.ds(i * n_rows + r, step), pl.ds(at + j * LANES, LANES)] = (
                    (upper + upper - lower) * inverse
                ).astype(abuf.dtype)
                abuf[pl.ds(j * n_rows + r, step), pl.ds(at + i * LANES, LANES)] = (
                    (lower + lower - upper) * inverse
                ).astype(abuf.dtype)

    span = min(n_occ, max(1, 1024 // aux))
    spans = [(s, span) for s in range(0, n_occ - span, span)]
    tail = max(1, span // 2)
    spans += [(s, tail) for s in range(n_occ - span, n_occ, tail)]
    flags = list(held)
    sent = []
    for number, (low, high, chosen) in enumerate(jobs):
        first_row, n_rows = low * part, (high - low) * part
        for c in needed_rows((low, high)):
            for made in row_copies.pop(c, ()):
                made.wait()
        for slot, unit in enumerate(chosen):
            index = units.index(unit)
            for j in range(CAP + 1):
                for made in col_copies.pop((unit, j), ()):
                    made.wait()
                if number == 0 and slot == 0 and j == 2:
                    total_copies = [
                        copy(before.at[:, pl.ds(a * part, (b - a) * part)], total.at[:, pl.ds(a * part, (b - a) * part)])
                        for a, b, flag in runs(held, 0, n_parts)
                        if flag
                    ]
                if j < CAP:
                    left = jnp.concatenate(
                        [
                            rows[s, :, first_row : first_row + n_rows].reshape(CAP * n_rows, aux)
                            for s in range(n_occ)
                        ],
                        axis=1,
                    )
                    right = jnp.concatenate([cols[index, s, j] for s in range(n_occ)], axis=1)
                    kbuf[j, pl.ds(0, CAP * n_rows)] = lax.dot_general(
                        left, right, (((1,), (1,)), ((), ())), preferred_element_type=jnp.float32
                    )
                for i in range(j):
                    combine(first_row, n_rows, unit, slot * CAP * LANES, i, j - 1)
        if number == 0:
            for made in total_copies:
                made.wait()
        depth = len(chosen) * CAP * LANES
        for s, span in spans:
            lanes = pl.ds(s * aux, span * aux)
            right = jnp.concatenate(
                [
                    jnp.concatenate(
                        [cols[units.index(unit), t].reshape(CAP * LANES, aux) for unit in chosen],
                        axis=0,
                    )
                    for t in range(s, s + span)
                ],
                axis=1,
            )
            added = jnp.dot(
                abuf[pl.ds(0, CAP * n_rows), pl.ds(0, depth)], right, preferred_element_type=jnp.float32
            ).reshape(CAP, n_rows, span * aux)
            final = number == len(jobs) - 1
            for a, b, flag in runs(flags, low, high):
                where = pl.ds(a * part, (b - a) * part)
                piece = added[:, (a - low) * part : (b - low) * part]
                if flag:
                    piece = piece + total[:, where, lanes]
                if last and final:
                    result[:, where, lanes] = piece.astype(result.dtype)
                else:
                    total[:, where, lanes] = piece
            if final:
                if last:
                    for t in range(s, s + span):
                        place = pl.multiple_of((me[0] ^ t) * aux, aux)
                        sent.append(
                            copy(result.at[:, :, pl.ds(t * aux, aux)], out.at[:, :, pl.ds(place, aux)])
                        )
                else:
                    for a, b, flag in runs(
                        [f or low <= p < high for p, f in enumerate(flags)], 0, n_parts
                    ):
                        where = pl.ds(a * part, (b - a) * part)
                        if flag:
                            sent.append(
                                copy(total.at[:, where, lanes], out.at[:, where, lanes])
                            )
        flags = [f or low <= p < high for p, f in enumerate(flags)]
    for made in sent:
        made.wait()


def chunk_of(cuts, unit):
    return next(c for c in range(len(cuts)) if unit < sum(cuts[: c + 1]))


def plan(cuts, jobs):
    units = []
    for _, _, chosen in jobs:
        units += [unit for unit in chosen if unit not in units]
    chunks = sorted({chunk_of(cuts, unit) for unit in units})
    rows = sorted({chunk_of(cuts, p) for low, high, _ in jobs for p in range(low, high)})
    return units, chunks, rows


def density(token, scalars, first_blocks, blocks, before, held, jobs, last, cuts):
    n_blocks = len(first_blocks)
    width, aux = first_blocks[0].shape[1:]
    part = width // sum(cuts)
    n_occ = blocks[0][0].shape[0] + 1
    naux = n_occ * aux
    units, chunks, row_chunks = plan(cuts, jobs)
    kept = jnp.bfloat16 if last else jnp.float32
    deepest = max(len(chosen) for _, _, chosen in jobs)
    tallest = max(high - low for low, high, _ in jobs) * part * CAP
    operands = [*scalars, token, *first_blocks]
    for c in chunks:
        operands += blocks[c]
    operands += [blocks[c][0] for c in row_chunks if c not in chunks]
    operands += [before] if any(held) else []
    at = len(scalars)
    done = pl.pallas_call(
        functools.partial(density_kernel, n_occ, n_blocks, cuts, jobs, held, last),
        out_shape=[
            jax.ShapeDtypeStruct(token.shape, token.dtype),
            jax.ShapeDtypeStruct((CAP, width, naux), kept),
        ],
        in_specs=[ANY] * len(operands),
        out_specs=[ANY] * 2,
        scratch_shapes=[
            *[pltpu.SMEM(x.shape, x.dtype) for x in scalars[:4]],
            *[pltpu.VMEM(x.shape, x.dtype) for x in scalars[4:]],
            pltpu.VMEM((n_occ, CAP, width, aux), jnp.bfloat16),
            pltpu.VMEM((len(units), n_occ, CAP, LANES, aux), jnp.bfloat16),
            pltpu.VMEM((CAP, tallest, LANES), jnp.float32),
            pltpu.VMEM((tallest, deepest * CAP * LANES), jnp.bfloat16),
            pltpu.VMEM((CAP, width, naux), jnp.float32),
            pltpu.VMEM((CAP, width, naux) if last else (1, 16, 128), jnp.bfloat16),
            pltpu.SemaphoreType.DMA((48 + 2 * n_blocks * (len(units) + 4),)),
        ],
        input_output_aliases={at: 0},
        compiler_params=pltpu.CompilerParams(vmem_limit_bytes=VMEM_LIMIT),
        cost_estimate=SMALL,
    )(*operands)
    held = tuple(
        f or any(low <= p < high for low, high, _ in jobs) for p, f in enumerate(held)
    )
    return done[0], done[1], held


def on_device(basis, group_sizes, orbital_order, eps_occ, eps_vir):
    n_virt, n_occ = lax.axis_size("virt"), lax.axis_size("occ")
    me_occ, me_virt = lax.axis_index("occ"), lax.axis_index("virt")
    width, aux = basis.shape[1:]
    dims = (n_virt // 2).bit_length() - 1
    part = LANES // n_virt
    n_parts = width // part
    me = me_occ.reshape(1).astype(jnp.int32)
    n_own = 1 << dims

    def bit(dim, core):
        return 2 << ((dim + core) % dims)

    def hop(block, dim):
        pairs = [(d, d ^ bit(dim, d & 1)) for d in range(n_virt)]
        return lax.ppermute(block, "virt", pairs)

    def sibling(block):
        return lax.ppermute(block, "virt", [(d, d ^ 1) for d in range(n_virt)])

    def across(block, mask):
        return lax.ppermute(block, "occ", [(d, d ^ mask) for d in range(n_occ)])

    def origin(mask, core):
        return sum(bit(dim, core) for dim in range(dims) if mask >> dim & 1)

    core = me_virt & 1
    origins = [
        me_virt ^ jnp.where(core == 0, origin(m, 0), origin(m, 1)) for m in range(n_own)
    ] + [
        me_virt ^ 1 ^ jnp.where(core == 0, origin(m, 1), origin(m, 0)) for m in range(n_own)
    ]
    by_owner = eps_vir.reshape(n_virt, n_parts, part)
    vb = by_owner[jnp.stack(origins)].transpose(1, 0, 2).reshape(n_parts, 1, LANES)
    va = lax.dynamic_slice_in_dim(eps_vir, me_virt * width, width).reshape(width, 1)
    scalars = (me, group_sizes, orbital_order, eps_occ, va, vb)

    z_parts = (1, 2, 2)
    cuts = z_parts
    starts = [sum(cuts[:c]) * part for c in range(len(cuts) + 1)]
    sends = []
    token, send, first = stage(None, basis, *scalars[:3], n_occ, 0, starts[1], with_own=True)
    sends.append([send])
    blocks = {}

    def spread(name, block):
        held = blocks[name] = [block] + [None] * (2 * n_own - 1)
        held[n_own] = sibling(block)
        for dim in range(dims):
            held[1 << dim] = hop(block, dim)

    def relay(token, name, level):
        held = blocks[name]
        arrived = [m for m in range(1, n_own) if m.bit_count() == level]
        token, gated = gate(token, (), [held[m] for m in arrived])
        for m, block in zip(arrived, gated):
            held[m] = block
        for m in arrived:
            for dim in range(m.bit_length(), dims):
                held[m | 1 << dim] = hop(held[m], dim)
        for m in arrived:
            held[n_own + m] = sibling(held[m])
        return token

    crossing = []
    n_chunks = len(z_parts)

    def cross(token, c):
        token, gated = gate(token, (), sends[c])
        if len(gated) == 1:
            crossing.append([lax.all_to_all(gated[0], "occ", 0, 0, tiled=True)])
        else:
            crossing.append([across(block, mask) for mask, block in enumerate(gated, 1)])
        return token

    total, held = None, (False,) * n_parts

    def add(jobs, last=False):
        nonlocal token, total, held
        token, total, held = density(
            token, scalars, blocks["first"], chunks, total, held, jobs, last, cuts
        )

    def arrive(name):
        nonlocal token
        for level in range(2, dims + 1):
            token = relay(token, name, level)

    chunks = {}

    def collect(c):
        nonlocal token
        token, (block,) = join(token, me, crossing[c], 1)
        spread(c, block)
        chunks[c] = blocks[c]

    token = cross(token, 0)
    spread("first", first)
    for c in range(1, n_chunks):
        token, *send = stage(token, basis, *scalars[:3], n_occ, starts[c], starts[c + 1])
        sends.append(send)
    for c in range(1, n_chunks):
        token = cross(token, c)
    token, _ = gate(token, (va, vb))
    collect(0)
    token = relay(token, "first", 1)
    arrive("first")
    token = relay(token, 0, 1)
    collect(1)
    arrive(0)
    early = cuts[0] + cuts[1]
    add([(0, early, (0,))])
    token = relay(token, 1, 1)
    collect(2)
    arrive(1)
    add([(early, n_parts, (0,)), (0, n_parts, (1,))])
    token = relay(token, 2, 1)
    add([(0, n_parts, (2,))])
    arrive(2)
    add([(0, n_parts, (3, 4))], True)
    return total.reshape(1, CAP, width, n_occ * aux)


def solution(mesh):
    return jax.shard_map(
        on_device,
        mesh=mesh,
        in_specs=(P(None, "virt", "occ"), P(), P(), P(), P()),
        out_specs=P("occ", None, "virt", None),
        check_vma=False,
    )
```

```python
import functools

import jax
import jax.numpy as jnp
from jax import lax
from jax.experimental import pallas as pl
from jax.experimental.pallas import tpu as pltpu
from jax.sharding import PartitionSpec as P

CAP = 6
LANES = 256
VMEM_LIMIT = (64 << 20) - (512 << 10)
SMALL = pl.CostEstimate(flops=1 << 10, bytes_accessed=1 << 10, transcendentals=0)
ANY = pl.BlockSpec(memory_space=pl.ANY)
VMEM = pl.BlockSpec(memory_space=pltpu.VMEM)
SMEM = pl.BlockSpec(memory_space=pltpu.SMEM)


def group_slots(sizes, order, group, n_groups):
    offset = jnp.int32(0)
    count = jnp.int32(0)
    for other in range(n_groups):
        offset = offset + jnp.where(other < group, sizes[other], 0)
        count = count + jnp.where(other == group, sizes[other], 0)
    last = order.shape[0] - 1
    return [
        (order[jnp.minimum(offset + slot, last)], slot < count) for slot in range(CAP)
    ]


def stage_kernel(n_occ, low, high, with_own, split, me, sizes, order, basis, *refs):
    refs = refs if with_own else refs[1:]
    outs, own, (held, read, sent) = refs[1:-3], refs[-4], refs[-3:]
    if with_own:
        refs[0][...] = jnp.zeros(refs[0].shape, refs[0].dtype)
    reads = []
    copies = []
    rows = pl.ds(low, high - low)
    for mask in range(n_occ):
        whole = with_own and mask == 0
        for slot, (orbital, live) in enumerate(
            group_slots(sizes, order, me[0] ^ mask, n_occ)
        ):
            index = mask * CAP + slot
            if whole:
                copy = pltpu.make_async_copy(basis.at[orbital], held.at[0, slot], read.at[index])
            else:
                copy = pltpu.make_async_copy(
                    basis.at[orbital, rows], held.at[mask, slot, pl.ds(0, high - low)], read.at[index]
                )
            copy.start()
            reads.append((copy, live))
    for mask in range(n_occ):
        for slot in range(CAP):
            copy, live = reads[mask * CAP + slot]
            copy.wait()

            @pl.when(jnp.logical_not(live))
            def _():
                held[mask, slot] = jnp.zeros(held.shape[2:], held.dtype)

        if mask or not split:
            target = outs[mask - 1] if split else outs[0].at[me[0] ^ mask]
            copies.append(
                pltpu.make_async_copy(held.at[mask, :, pl.ds(0, high - low)], target, sent.at[mask])
            )
            copies[-1].start()
        if with_own and mask == 0:
            copies.append(pltpu.make_async_copy(held.at[0], own, sent.at[n_occ]))
            copies[-1].start()
    for copy in copies:
        copy.wait()


def stage(token, basis, me, sizes, order, n_occ, low, high, with_own=False, split=False):
    width, aux = basis.shape[1:]
    piece = (CAP, high - low, aux)
    shapes = [piece] * (n_occ - 1) if split else [(n_occ, *piece)]
    shapes += [(CAP, width, aux)] * with_own
    return pl.pallas_call(
        functools.partial(stage_kernel, n_occ, low, high, with_own, split),
        out_shape=[
            jax.ShapeDtypeStruct((8, 128), jnp.float32),
            *[jax.ShapeDtypeStruct(shape, basis.dtype) for shape in shapes],
        ],
        in_specs=[SMEM, SMEM, SMEM, ANY] + [ANY] * (not with_own),
        out_specs=[VMEM if with_own else ANY] + [ANY] * len(shapes),
        scratch_shapes=[
            pltpu.VMEM((n_occ, CAP, width if with_own else high - low, aux), basis.dtype),
            pltpu.SemaphoreType.DMA((n_occ * CAP,)),
            pltpu.SemaphoreType.DMA((1 + n_occ,)),
        ],
        input_output_aliases={} if with_own else {4: 0},
        compiler_params=pltpu.CompilerParams(vmem_limit_bytes=VMEM_LIMIT),
        cost_estimate=SMALL,
    )(me, sizes, order, basis, *([] if with_own else [token]))


def gate(token, needs=(), gives=()):
    operands = [token, *gives, *needs]
    kept = 1 + len(gives)
    done = pl.pallas_call(
        lambda *refs: None,
        out_shape=[jax.ShapeDtypeStruct(x.shape, x.dtype) for x in operands[:kept]],
        in_specs=[ANY] * len(operands),
        out_specs=[ANY] * kept,
        input_output_aliases={i: i for i in range(kept)},
        compiler_params=pltpu.CompilerParams(vmem_limit_bytes=VMEM_LIMIT),
        cost_estimate=SMALL,
    )(*operands)
    return done[0], done[1:]


def join_kernel(n_occ, n_got, parts, me, token_in, *refs):
    got, outs, (held, read, sent) = refs[:n_got], refs[n_got + 1 : -3], refs[-3:]
    sources = got if n_got > 1 else [got[0].at[me[0] ^ mask] for mask in range(1, n_occ)]
    reads = [
        pltpu.make_async_copy(source, held.at[i], read.at[i]) for i, source in enumerate(sources)
    ]
    width = held.shape[2] // parts
    for copy in reads:
        copy.start()
    sends = []
    for i, copy in enumerate(reads):
        copy.wait()
        for p in range(parts):
            sends.append(
                pltpu.make_async_copy(
                    held.at[i, :, pl.ds(p * width, width)], outs[p].at[i], sent.at[len(sends)]
                )
            )
            sends[-1].start()
    for copy in sends:
        copy.wait()


def join(token, me, got, parts):
    cap, rows, aux = got[0].shape[-3:]
    n_occ = got[0].shape[0] if len(got) == 1 else len(got) + 1
    shape = jax.ShapeDtypeStruct((n_occ - 1, cap, rows // parts, aux), got[0].dtype)
    done = pl.pallas_call(
        functools.partial(join_kernel, n_occ, len(got), parts),
        out_shape=[jax.ShapeDtypeStruct(token.shape, token.dtype)] + [shape] * parts,
        in_specs=[SMEM] + [ANY] * (1 + len(got)),
        out_specs=[ANY] * (1 + parts),
        scratch_shapes=[
            pltpu.VMEM((n_occ - 1, cap, rows, aux), got[0].dtype),
            pltpu.SemaphoreType.DMA((n_occ,)),
            pltpu.SemaphoreType.DMA((parts * (n_occ - 1),)),
        ],
        input_output_aliases={1: 0},
        compiler_params=pltpu.CompilerParams(vmem_limit_bytes=VMEM_LIMIT),
        cost_estimate=SMALL,
    )(me, token, *got)
    return done[0], done[1:]


def runs(flags, low, high):
    out = []
    for p in range(low, high):
        if out and flags[p] == out[-1][2]:
            out[-1] = (out[-1][0], p + 1, flags[p])
        else:
            out.append((p, p + 1, flags[p]))
    return out


def density_kernel(
    n_occ, n_blocks, cuts, jobs, held, last, *refs
):
    refs = list(refs)
    small = [refs.pop(0) for _ in range(6)]
    refs.pop(0)
    n_parts = sum(cuts)
    first_blocks = [refs.pop(0) for _ in range(n_blocks)]
    units, chunks, row_chunks = plan(cuts, jobs)
    col_blocks = {c: [refs.pop(0) for _ in range(n_blocks)] for c in chunks}
    own = {c: col_blocks[c][0] if c in chunks else refs.pop(0) for c in row_chunks}
    before = refs.pop(0) if any(held) else None
    refs.pop(0)
    out, me, sizes, order, eps_occ, va, vb, rows, cols, kbuf, abuf, total, result, sems = refs
    width, aux = rows.shape[2], rows.shape[3]
    part = width // n_parts
    n_copies = 0

    def copy(source, target):
        nonlocal n_copies
        made = pltpu.make_async_copy(source, target, sems.at[n_copies])
        made.start()
        n_copies += 1
        return made

    small_copies = [copy(a, b) for a, b in zip(small, (me, sizes, order, eps_occ, va, vb))]

    def load_rows(c):
        place = pl.ds(sum(cuts[:c]) * part, cuts[c] * part)
        return [
            copy(first_blocks[0].at[:, place], rows.at[0, :, place]),
            copy(own[c], rows.at[pl.ds(1, n_occ - 1), :, place]),
        ]

    def load_cols(unit, first, count):
        index, slots = units.index(unit), pl.ds(first, count)
        c = chunk_of(cuts, unit)
        inside = pl.ds((unit - sum(cuts[:c])) * part, part)
        copies = []
        for b in range(n_blocks):
            place = pl.ds(b * part, part)
            copies.append(
                copy(
                    first_blocks[b].at[slots, pl.ds(unit * part, part)],
                    cols.at[index, 0, slots, place],
                )
            )
            copies.append(
                copy(
                    col_blocks[c][b].at[:, slots, inside],
                    cols.at[index, pl.ds(1, n_occ - 1), slots, place],
                )
            )
        return copies

    def needed_rows(job):
        return [c for c in row_chunks if job[0] < sum(cuts[: c + 1]) and sum(cuts[:c]) < job[1]]

    row_copies = {c: load_rows(c) for c in needed_rows(jobs[0])}
    col_copies = {
        (units[0], first): load_cols(units[0], first, count)
        for first, count in ((0, 2), (2, 2), (4, 2))
    }
    for c in row_chunks:
        if c not in row_copies:
            row_copies[c] = load_rows(c)
    for unit in units[1:]:
        col_copies[unit, 0] = load_cols(unit, 0, CAP)
    total_copies = []
    for made in small_copies:
        made.wait()
    energy = []
    for orbital, live in group_slots(sizes, order, me[0], n_occ):
        energy.append(jnp.where(live, eps_occ[orbital], jnp.float32(0.0)))

    def combine(low, n_rows, unit, at, i, j):
        step = 32 if n_rows % 32 == 0 else 16
        for r in range(0, n_rows, step):
            gap = (energy[i] + energy[j]) - (va[pl.ds(low + r, step), :] + vb[unit])
            inverse = pltpu.reciprocal(gap, approx=True)
            inverse = inverse * (2.0 - gap * inverse)
            upper = kbuf[j, pl.ds(i * n_rows + r, step), :]
            if i == j:
                abuf[pl.ds(i * n_rows + r, step), pl.ds(at + j * LANES, LANES)] = (
                    upper * inverse
                ).astype(abuf.dtype)
            else:
                lower = kbuf[i, pl.ds(j * n_rows + r, step), :]
                abuf[pl.ds(i * n_rows + r, step), pl.ds(at + j * LANES, LANES)] = (
                    (upper + upper - lower) * inverse
                ).astype(abuf.dtype)
                abuf[pl.ds(j * n_rows + r, step), pl.ds(at + i * LANES, LANES)] = (
                    (lower + lower - upper) * inverse
                ).astype(abuf.dtype)

    span = min(n_occ, max(1, 1024 // aux))
    spans = [(s, span) for s in range(0, n_occ - span, span)]
    tail = max(1, span // 2)
    spans += [(s, tail) for s in range(n_occ - span, n_occ, tail)]
    flags = list(held)
    sent = []
    for number, (low, high, chosen) in enumerate(jobs):
        first_row, n_rows = low * part, (high - low) * part
        for c in needed_rows((low, high)):
            for made in row_copies.pop(c, ()):
                made.wait()
        for slot, unit in enumerate(chosen):
            index = units.index(unit)
            for j in range(CAP + 1):
                for made in col_copies.pop((unit, j), ()):
                    made.wait()
                if number == 0 and slot == 0 and j == 2:
                    total_copies = [
                        copy(before.at[:, pl.ds(a * part, (b - a) * part)], total.at[:, pl.ds(a * part, (b - a) * part)])
                        for a, b, flag in runs(held, 0, n_parts)
                        if flag
                    ]
                if j < CAP:
                    left = jnp.concatenate(
                        [
                            rows[s, :, first_row : first_row + n_rows].reshape(CAP * n_rows, aux)
                            for s in range(n_occ)
                        ],
                        axis=1,
                    )
                    right = jnp.concatenate([cols[index, s, j] for s in range(n_occ)], axis=1)
                    kbuf[j, pl.ds(0, CAP * n_rows)] = lax.dot_general(
                        left, right, (((1,), (1,)), ((), ())), preferred_element_type=jnp.float32
                    )
                for i in range(j):
                    combine(first_row, n_rows, unit, slot * CAP * LANES, i, j - 1)
        if number == 0:
            for made in total_copies:
                made.wait()
        depth = len(chosen) * CAP * LANES
        for s, span in spans:
            lanes = pl.ds(s * aux, span * aux)
            right = jnp.concatenate(
                [
                    jnp.concatenate(
                        [cols[units.index(unit), t].reshape(CAP * LANES, aux) for unit in chosen],
                        axis=0,
                    )
                    for t in range(s, s + span)
                ],
                axis=1,
            )
            added = jnp.dot(
                abuf[pl.ds(0, CAP * n_rows), pl.ds(0, depth)], right, preferred_element_type=jnp.float32
            ).reshape(CAP, n_rows, span * aux)
            final = number == len(jobs) - 1
            for a, b, flag in runs(flags, low, high):
                where = pl.ds(a * part, (b - a) * part)
                piece = added[:, (a - low) * part : (b - low) * part]
                if flag:
                    piece = piece + total[:, where, lanes]
                if last and final:
                    result[:, where, lanes] = piece.astype(result.dtype)
                else:
                    total[:, where, lanes] = piece
            if final:
                if last:
                    for t in range(s, s + span):
                        place = pl.multiple_of((me[0] ^ t) * aux, aux)
                        sent.append(
                            copy(result.at[:, :, pl.ds(t * aux, aux)], out.at[:, :, pl.ds(place, aux)])
                        )
                else:
                    for a, b, flag in runs(
                        [f or low <= p < high for p, f in enumerate(flags)], 0, n_parts
                    ):
                        where = pl.ds(a * part, (b - a) * part)
                        if flag:
                            sent.append(
                                copy(total.at[:, where, lanes], out.at[:, where, lanes])
                            )
        flags = [f or low <= p < high for p, f in enumerate(flags)]
    for made in sent:
        made.wait()


def chunk_of(cuts, unit):
    return next(c for c in range(len(cuts)) if unit < sum(cuts[: c + 1]))


def plan(cuts, jobs):
    units = []
    for _, _, chosen in jobs:
        units += [unit for unit in chosen if unit not in units]
    chunks = sorted({chunk_of(cuts, unit) for unit in units})
    rows = sorted({chunk_of(cuts, p) for low, high, _ in jobs for p in range(low, high)})
    return units, chunks, rows


def density(token, scalars, first_blocks, blocks, before, held, jobs, last, cuts):
    n_blocks = len(first_blocks)
    width, aux = first_blocks[0].shape[1:]
    part = width // sum(cuts)
    n_occ = blocks[0][0].shape[0] + 1
    naux = n_occ * aux
    units, chunks, row_chunks = plan(cuts, jobs)
    kept = jnp.bfloat16 if last else jnp.float32
    deepest = max(len(chosen) for _, _, chosen in jobs)
    tallest = max(high - low for low, high, _ in jobs) * part * CAP
    operands = [*scalars, token, *first_blocks]
    for c in chunks:
        operands += blocks[c]
    operands += [blocks[c][0] for c in row_chunks if c not in chunks]
    operands += [before] if any(held) else []
    at = len(scalars)
    done = pl.pallas_call(
        functools.partial(density_kernel, n_occ, n_blocks, cuts, jobs, held, last),
        out_shape=[
            jax.ShapeDtypeStruct(token.shape, token.dtype),
            jax.ShapeDtypeStruct((CAP, width, naux), kept),
        ],
        in_specs=[ANY] * len(operands),
        out_specs=[ANY] * 2,
        scratch_shapes=[
            *[pltpu.SMEM(x.shape, x.dtype) for x in scalars[:4]],
            *[pltpu.VMEM(x.shape, x.dtype) for x in scalars[4:]],
            pltpu.VMEM((n_occ, CAP, width, aux), jnp.bfloat16),
            pltpu.VMEM((len(units), n_occ, CAP, LANES, aux), jnp.bfloat16),
            pltpu.VMEM((CAP, tallest, LANES), jnp.float32),
            pltpu.VMEM((tallest, deepest * CAP * LANES), jnp.bfloat16),
            pltpu.VMEM((CAP, width, naux), jnp.float32),
            pltpu.VMEM((CAP, width, naux) if last else (1, 16, 128), jnp.bfloat16),
            pltpu.SemaphoreType.DMA((48 + 2 * n_blocks * (len(units) + 4),)),
        ],
        input_output_aliases={at: 0},
        compiler_params=pltpu.CompilerParams(vmem_limit_bytes=VMEM_LIMIT),
        cost_estimate=SMALL,
    )(*operands)
    held = tuple(
        f or any(low <= p < high for low, high, _ in jobs) for p, f in enumerate(held)
    )
    return done[0], done[1], held


def on_device(basis, group_sizes, orbital_order, eps_occ, eps_vir):
    n_virt, n_occ = lax.axis_size("virt"), lax.axis_size("occ")
    me_occ, me_virt = lax.axis_index("occ"), lax.axis_index("virt")
    width, aux = basis.shape[1:]
    dims = (n_virt // 2).bit_length() - 1
    part = LANES // n_virt
    n_parts = width // part
    me = me_occ.reshape(1).astype(jnp.int32)
    n_own = 1 << dims

    def bit(dim, core):
        return 2 << ((dim + core) % dims)

    def hop(block, dim):
        pairs = [(d, d ^ bit(dim, d & 1)) for d in range(n_virt)]
        return lax.ppermute(block, "virt", pairs)

    def sibling(block):
        return lax.ppermute(block, "virt", [(d, d ^ 1) for d in range(n_virt)])

    def across(block, mask):
        return lax.ppermute(block, "occ", [(d, d ^ mask) for d in range(n_occ)])

    def origin(mask, core):
        return sum(bit(dim, core) for dim in range(dims) if mask >> dim & 1)

    core = me_virt & 1
    origins = [
        me_virt ^ jnp.where(core == 0, origin(m, 0), origin(m, 1)) for m in range(n_own)
    ] + [
        me_virt ^ 1 ^ jnp.where(core == 0, origin(m, 1), origin(m, 0)) for m in range(n_own)
    ]
    by_owner = eps_vir.reshape(n_virt, n_parts, part)
    vb = by_owner[jnp.stack(origins)].transpose(1, 0, 2).reshape(n_parts, 1, LANES)
    va = lax.dynamic_slice_in_dim(eps_vir, me_virt * width, width).reshape(width, 1)
    scalars = (me, group_sizes, orbital_order, eps_occ, va, vb)

    z_parts = (1, 2, 2)
    cuts = z_parts
    starts = [sum(cuts[:c]) * part for c in range(len(cuts) + 1)]
    sends = []
    token, send, first = stage(None, basis, *scalars[:3], n_occ, 0, starts[1], with_own=True)
    sends.append([send])
    blocks = {}

    def spread(name, block):
        held = blocks[name] = [block] + [None] * (2 * n_own - 1)
        held[n_own] = sibling(block)
        for dim in range(dims):
            held[1 << dim] = hop(block, dim)

    def relay(token, name, level):
        held = blocks[name]
        arrived = [m for m in range(1, n_own) if m.bit_count() == level]
        token, gated = gate(token, (), [held[m] for m in arrived])
        for m, block in zip(arrived, gated):
            held[m] = block
        for m in arrived:
            for dim in range(m.bit_length(), dims):
                held[m | 1 << dim] = hop(held[m], dim)
        for m in arrived:
            held[n_own + m] = sibling(held[m])
        return token

    crossing = []
    n_chunks = len(z_parts)

    def cross(token, c):
        token, gated = gate(token, (), sends[c])
        if len(gated) == 1:
            crossing.append([lax.all_to_all(gated[0], "occ", 0, 0, tiled=True)])
        else:
            crossing.append([across(block, mask) for mask, block in enumerate(gated, 1)])
        return token

    total, held = None, (False,) * n_parts

    def add(jobs, last=False):
        nonlocal token, total, held
        token, total, held = density(
            token, scalars, blocks["first"], chunks, total, held, jobs, last, cuts
        )

    def arrive(name):
        nonlocal token
        for level in range(2, dims + 1):
            token = relay(token, name, level)

    chunks = {}

    def collect(c):
        nonlocal token
        token, (block,) = join(token, me, crossing[c], 1)
        spread(c, block)
        chunks[c] = blocks[c]

    token = cross(token, 0)
    spread("first", first)
    for c in range(1, n_chunks):
        token, *send = stage(token, basis, *scalars[:3], n_occ, starts[c], starts[c + 1])
        sends.append(send)
    for c in range(1, n_chunks):
        token = cross(token, c)
    token, _ = gate(token, (va, vb))
    collect(0)
    token = relay(token, "first", 1)
    arrive("first")
    token = relay(token, 0, 1)
    collect(1)
    arrive(0)
    early = cuts[0] + cuts[1]
    add([(0, early, (0,))])
    token = relay(token, 1, 1)
    collect(2)
    arrive(1)
    add([(0, n_parts, (1,)), (early, n_parts, (0,))])
    token = relay(token, 2, 1)
    add([(0, n_parts, (2,))])
    arrive(2)
    add([(0, n_parts, (3, 4))], True)
    return total.reshape(1, CAP, width, n_occ * aux)


def solution(mesh):
    return jax.shard_map(
        on_device,
        mesh=mesh,
        in_specs=(P(None, "virt", "occ"), P(), P(), P(), P()),
        out_specs=P("occ", None, "virt", None),
        check_vma=False,
    )
```

```python
import functools

import jax
import jax.numpy as jnp
from jax import lax
from jax.experimental import pallas as pl
from jax.experimental.pallas import tpu as pltpu
from jax.sharding import PartitionSpec as P

CAP = 6
LANES = 256
VMEM_LIMIT = (64 << 20) - (512 << 10)
SMALL = pl.CostEstimate(flops=1 << 10, bytes_accessed=1 << 10, transcendentals=0)
ANY = pl.BlockSpec(memory_space=pl.ANY)
VMEM = pl.BlockSpec(memory_space=pltpu.VMEM)
SMEM = pl.BlockSpec(memory_space=pltpu.SMEM)


def group_slots(sizes, order, group, n_groups):
    offset = jnp.int32(0)
    count = jnp.int32(0)
    for other in range(n_groups):
        offset = offset + jnp.where(other < group, sizes[other], 0)
        count = count + jnp.where(other == group, sizes[other], 0)
    last = order.shape[0] - 1
    return [
        (order[jnp.minimum(offset + slot, last)], slot < count) for slot in range(CAP)
    ]


def stage_kernel(n_occ, low, high, with_own, split, me, sizes, order, basis, *refs):
    refs = refs if with_own else refs[1:]
    outs, own, (held, read, sent) = refs[1:-3], refs[-4], refs[-3:]
    if with_own:
        refs[0][...] = jnp.zeros(refs[0].shape, refs[0].dtype)
    reads = []
    copies = []
    rows = pl.ds(low, high - low)
    for mask in range(n_occ):
        whole = with_own and mask == 0
        for slot, (orbital, live) in enumerate(
            group_slots(sizes, order, me[0] ^ mask, n_occ)
        ):
            index = mask * CAP + slot
            if whole:
                copy = pltpu.make_async_copy(basis.at[orbital], held.at[0, slot], read.at[index])
            else:
                copy = pltpu.make_async_copy(
                    basis.at[orbital, rows], held.at[mask, slot, pl.ds(0, high - low)], read.at[index]
                )
            copy.start()
            reads.append((copy, live))
    for mask in range(n_occ):
        for slot in range(CAP):
            copy, live = reads[mask * CAP + slot]
            copy.wait()

            @pl.when(jnp.logical_not(live))
            def _():
                held[mask, slot] = jnp.zeros(held.shape[2:], held.dtype)

        if mask or not split:
            target = outs[mask - 1] if split else outs[0].at[me[0] ^ mask]
            copies.append(
                pltpu.make_async_copy(held.at[mask, :, pl.ds(0, high - low)], target, sent.at[mask])
            )
            copies[-1].start()
        if with_own and mask == 0:
            copies.append(pltpu.make_async_copy(held.at[0], own, sent.at[n_occ]))
            copies[-1].start()
    for copy in copies:
        copy.wait()


def stage(token, basis, me, sizes, order, n_occ, low, high, with_own=False, split=False):
    width, aux = basis.shape[1:]
    piece = (CAP, high - low, aux)
    shapes = [piece] * (n_occ - 1) if split else [(n_occ, *piece)]
    shapes += [(CAP, width, aux)] * with_own
    return pl.pallas_call(
        functools.partial(stage_kernel, n_occ, low, high, with_own, split),
        out_shape=[
            jax.ShapeDtypeStruct((8, 128), jnp.float32),
            *[jax.ShapeDtypeStruct(shape, basis.dtype) for shape in shapes],
        ],
        in_specs=[SMEM, SMEM, SMEM, ANY] + [ANY] * (not with_own),
        out_specs=[VMEM if with_own else ANY] + [ANY] * len(shapes),
        scratch_shapes=[
            pltpu.VMEM((n_occ, CAP, width if with_own else high - low, aux), basis.dtype),
            pltpu.SemaphoreType.DMA((n_occ * CAP,)),
            pltpu.SemaphoreType.DMA((1 + n_occ,)),
        ],
        input_output_aliases={} if with_own else {4: 0},
        compiler_params=pltpu.CompilerParams(vmem_limit_bytes=VMEM_LIMIT),
        cost_estimate=SMALL,
    )(me, sizes, order, basis, *([] if with_own else [token]))


def gate(token, needs=(), gives=()):
    operands = [token, *gives, *needs]
    kept = 1 + len(gives)
    done = pl.pallas_call(
        lambda *refs: None,
        out_shape=[jax.ShapeDtypeStruct(x.shape, x.dtype) for x in operands[:kept]],
        in_specs=[ANY] * len(operands),
        out_specs=[ANY] * kept,
        input_output_aliases={i: i for i in range(kept)},
        compiler_params=pltpu.CompilerParams(vmem_limit_bytes=VMEM_LIMIT),
        cost_estimate=SMALL,
    )(*operands)
    return done[0], done[1:]


def join_kernel(n_occ, n_got, parts, me, token_in, *refs):
    got, outs, (held, read, sent) = refs[:n_got], refs[n_got + 1 : -3], refs[-3:]
    sources = got if n_got > 1 else [got[0].at[me[0] ^ mask] for mask in range(1, n_occ)]
    reads = [
        pltpu.make_async_copy(source, held.at[i], read.at[i]) for i, source in enumerate(sources)
    ]
    width = held.shape[2] // parts
    for copy in reads:
        copy.start()
    sends = []
    for i, copy in enumerate(reads):
        copy.wait()
        for p in range(parts):
            sends.append(
                pltpu.make_async_copy(
                    held.at[i, :, pl.ds(p * width, width)], outs[p].at[i], sent.at[len(sends)]
                )
            )
            sends[-1].start()
    for copy in sends:
        copy.wait()


def join(token, me, got, parts):
    cap, rows, aux = got[0].shape[-3:]
    n_occ = got[0].shape[0] if len(got) == 1 else len(got) + 1
    shape = jax.ShapeDtypeStruct((n_occ - 1, cap, rows // parts, aux), got[0].dtype)
    done = pl.pallas_call(
        functools.partial(join_kernel, n_occ, len(got), parts),
        out_shape=[jax.ShapeDtypeStruct(token.shape, token.dtype)] + [shape] * parts,
        in_specs=[SMEM] + [ANY] * (1 + len(got)),
        out_specs=[ANY] * (1 + parts),
        scratch_shapes=[
            pltpu.VMEM((n_occ - 1, cap, rows, aux), got[0].dtype),
            pltpu.SemaphoreType.DMA((n_occ,)),
            pltpu.SemaphoreType.DMA((parts * (n_occ - 1),)),
        ],
        input_output_aliases={1: 0},
        compiler_params=pltpu.CompilerParams(vmem_limit_bytes=VMEM_LIMIT),
        cost_estimate=SMALL,
    )(me, token, *got)
    return done[0], done[1:]


def runs(flags, low, high):
    out = []
    for p in range(low, high):
        if out and flags[p] == out[-1][2]:
            out[-1] = (out[-1][0], p + 1, flags[p])
        else:
            out.append((p, p + 1, flags[p]))
    return out


def density_kernel(
    n_occ, n_blocks, cuts, jobs, held, last, *refs
):
    refs = list(refs)
    small = [refs.pop(0) for _ in range(6)]
    refs.pop(0)
    n_parts = sum(cuts)
    first_blocks = [refs.pop(0) for _ in range(n_blocks)]
    units, chunks, row_chunks = plan(cuts, jobs)
    col_blocks = {c: [refs.pop(0) for _ in range(n_blocks)] for c in chunks}
    own = {c: col_blocks[c][0] if c in chunks else refs.pop(0) for c in row_chunks}
    before = refs.pop(0) if any(held) else None
    refs.pop(0)
    out, me, sizes, order, eps_occ, va, vb, rows, cols, kbuf, abuf, total, result, sems = refs
    width, aux = rows.shape[2], rows.shape[3]
    part = width // n_parts
    n_copies = 0

    def copy(source, target):
        nonlocal n_copies
        made = pltpu.make_async_copy(source, target, sems.at[n_copies])
        made.start()
        n_copies += 1
        return made

    small_copies = [copy(a, b) for a, b in zip(small, (me, sizes, order, eps_occ, va, vb))]

    def load_rows(c):
        place = pl.ds(sum(cuts[:c]) * part, cuts[c] * part)
        return [
            copy(first_blocks[0].at[:, place], rows.at[0, :, place]),
            copy(own[c], rows.at[pl.ds(1, n_occ - 1), :, place]),
        ]

    def load_cols(unit, first, count):
        index, slots = units.index(unit), pl.ds(first, count)
        c = chunk_of(cuts, unit)
        inside = pl.ds((unit - sum(cuts[:c])) * part, part)
        copies = []
        for b in range(n_blocks):
            place = pl.ds(b * part, part)
            copies.append(
                copy(
                    first_blocks[b].at[slots, pl.ds(unit * part, part)],
                    cols.at[index, 0, slots, place],
                )
            )
            copies.append(
                copy(
                    col_blocks[c][b].at[:, slots, inside],
                    cols.at[index, pl.ds(1, n_occ - 1), slots, place],
                )
            )
        return copies

    def needed_rows(job):
        return [c for c in row_chunks if job[0] < sum(cuts[: c + 1]) and sum(cuts[:c]) < job[1]]

    row_copies = {c: load_rows(c) for c in needed_rows(jobs[0])}
    col_copies = {
        (units[0], first): load_cols(units[0], first, count)
        for first, count in ((0, 2), (2, 2), (4, 2))
    }
    for c in row_chunks:
        if c not in row_copies:
            row_copies[c] = load_rows(c)
    for unit in units[1:]:
        col_copies[unit, 0] = load_cols(unit, 0, CAP)
    total_copies = []
    for made in small_copies:
        made.wait()
    energy = []
    for orbital, live in group_slots(sizes, order, me[0], n_occ):
        energy.append(jnp.where(live, eps_occ[orbital], jnp.float32(0.0)))

    def combine(low, n_rows, unit, at, i, j):
        step = 32 if n_rows % 32 == 0 else 16
        for r in range(0, n_rows, step):
            gap = (energy[i] + energy[j]) - (va[pl.ds(low + r, step), :] + vb[unit])
            inverse = pltpu.reciprocal(gap, approx=True)
            inverse = inverse * (2.0 - gap * inverse)
            upper = kbuf[j, pl.ds(i * n_rows + r, step), :]
            if i == j:
                abuf[pl.ds(i * n_rows + r, step), pl.ds(at + j * LANES, LANES)] = (
                    upper * inverse
                ).astype(abuf.dtype)
            else:
                lower = kbuf[i, pl.ds(j * n_rows + r, step), :]
                abuf[pl.ds(i * n_rows + r, step), pl.ds(at + j * LANES, LANES)] = (
                    (upper + upper - lower) * inverse
                ).astype(abuf.dtype)
                abuf[pl.ds(j * n_rows + r, step), pl.ds(at + i * LANES, LANES)] = (
                    (lower + lower - upper) * inverse
                ).astype(abuf.dtype)

    span = min(n_occ, max(1, 1024 // aux))
    spans = [(s, span) for s in range(0, n_occ - span, span)]
    tail = max(1, span // 2)
    spans += [(s, tail) for s in range(n_occ - span, n_occ, tail)]
    flags = list(held)
    sent = []
    for number, (low, high, chosen) in enumerate(jobs):
        first_row, n_rows = low * part, (high - low) * part
        for c in needed_rows((low, high)):
            for made in row_copies.pop(c, ()):
                made.wait()
        for slot, unit in enumerate(chosen):
            index = units.index(unit)
            for j in range(CAP + 1):
                for made in col_copies.pop((unit, j), ()):
                    made.wait()
                if number == 0 and slot == 0 and j == 2:
                    total_copies = [
                        copy(before.at[:, pl.ds(a * part, (b - a) * part)], total.at[:, pl.ds(a * part, (b - a) * part)])
                        for a, b, flag in runs(held, 0, n_parts)
                        if flag
                    ]
                if j < CAP:
                    left = jnp.concatenate(
                        [
                            rows[s, :, first_row : first_row + n_rows].reshape(CAP * n_rows, aux)
                            for s in range(n_occ)
                        ],
                        axis=1,
                    )
                    right = jnp.concatenate([cols[index, s, j] for s in range(n_occ)], axis=1)
                    kbuf[j, pl.ds(0, CAP * n_rows)] = lax.dot_general(
                        left, right, (((1,), (1,)), ((), ())), preferred_element_type=jnp.float32
                    )
                for i in range(j):
                    combine(first_row, n_rows, unit, slot * CAP * LANES, i, j - 1)
        if number == 0:
            for made in total_copies:
                made.wait()
        depth = len(chosen) * CAP * LANES
        for s, span in spans:
            lanes = pl.ds(s * aux, span * aux)
            right = jnp.concatenate(
                [
                    jnp.concatenate(
                        [cols[units.index(unit), t].reshape(CAP * LANES, aux) for unit in chosen],
                        axis=0,
                    )
                    for t in range(s, s + span)
                ],
                axis=1,
            )
            added = jnp.dot(
                abuf[pl.ds(0, CAP * n_rows), pl.ds(0, depth)], right, preferred_element_type=jnp.float32
            ).reshape(CAP, n_rows, span * aux)
            final = number == len(jobs) - 1
            for a, b, flag in runs(flags, low, high):
                where = pl.ds(a * part, (b - a) * part)
                piece = added[:, (a - low) * part : (b - low) * part]
                if flag:
                    piece = piece + total[:, where, lanes]
                if last and final:
                    result[:, where, lanes] = piece.astype(result.dtype)
                else:
                    total[:, where, lanes] = piece
            if final:
                if last:
                    for t in range(s, s + span):
                        place = pl.multiple_of((me[0] ^ t) * aux, aux)
                        sent.append(
                            copy(result.at[:, :, pl.ds(t * aux, aux)], out.at[:, :, pl.ds(place, aux)])
                        )
                else:
                    for a, b, flag in runs(
                        [f or low <= p < high for p, f in enumerate(flags)], 0, n_parts
                    ):
                        where = pl.ds(a * part, (b - a) * part)
                        if flag:
                            sent.append(
                                copy(total.at[:, where, lanes], out.at[:, where, lanes])
                            )
        flags = [f or low <= p < high for p, f in enumerate(flags)]
    for made in sent:
        made.wait()


def chunk_of(cuts, unit):
    return next(c for c in range(len(cuts)) if unit < sum(cuts[: c + 1]))


def plan(cuts, jobs):
    units = []
    for _, _, chosen in jobs:
        units += [unit for unit in chosen if unit not in units]
    chunks = sorted({chunk_of(cuts, unit) for unit in units})
    rows = sorted({chunk_of(cuts, p) for low, high, _ in jobs for p in range(low, high)})
    return units, chunks, rows


def density(token, scalars, first_blocks, blocks, before, held, jobs, last, cuts):
    n_blocks = len(first_blocks)
    width, aux = first_blocks[0].shape[1:]
    part = width // sum(cuts)
    n_occ = blocks[0][0].shape[0] + 1
    naux = n_occ * aux
    units, chunks, row_chunks = plan(cuts, jobs)
    kept = jnp.bfloat16 if last else jnp.float32
    deepest = max(len(chosen) for _, _, chosen in jobs)
    tallest = max(high - low for low, high, _ in jobs) * part * CAP
    operands = [*scalars, token, *first_blocks]
    for c in chunks:
        operands += blocks[c]
    operands += [blocks[c][0] for c in row_chunks if c not in chunks]
    operands += [before] if any(held) else []
    at = len(scalars)
    done = pl.pallas_call(
        functools.partial(density_kernel, n_occ, n_blocks, cuts, jobs, held, last),
        out_shape=[
            jax.ShapeDtypeStruct(token.shape, token.dtype),
            jax.ShapeDtypeStruct((CAP, width, naux), kept),
        ],
        in_specs=[ANY] * len(operands),
        out_specs=[ANY] * 2,
        scratch_shapes=[
            *[pltpu.SMEM(x.shape, x.dtype) for x in scalars[:4]],
            *[pltpu.VMEM(x.shape, x.dtype) for x in scalars[4:]],
            pltpu.VMEM((n_occ, CAP, width, aux), jnp.bfloat16),
            pltpu.VMEM((len(units), n_occ, CAP, LANES, aux), jnp.bfloat16),
            pltpu.VMEM((CAP, tallest, LANES), jnp.float32),
            pltpu.VMEM((tallest, deepest * CAP * LANES), jnp.bfloat16),
            pltpu.VMEM((CAP, width, naux), jnp.float32),
            pltpu.VMEM((CAP, width, naux) if last else (1, 16, 128), jnp.bfloat16),
            pltpu.SemaphoreType.DMA((48 + 2 * n_blocks * (len(units) + 4),)),
        ],
        input_output_aliases={at: 0},
        compiler_params=pltpu.CompilerParams(vmem_limit_bytes=VMEM_LIMIT),
        cost_estimate=SMALL,
    )(*operands)
    held = tuple(
        f or any(low <= p < high for low, high, _ in jobs) for p, f in enumerate(held)
    )
    return done[0], done[1], held


def on_device(basis, group_sizes, orbital_order, eps_occ, eps_vir):
    n_virt, n_occ = lax.axis_size("virt"), lax.axis_size("occ")
    me_occ, me_virt = lax.axis_index("occ"), lax.axis_index("virt")
    width, aux = basis.shape[1:]
    dims = (n_virt // 2).bit_length() - 1
    part = LANES // n_virt
    n_parts = width // part
    me = me_occ.reshape(1).astype(jnp.int32)
    n_own = 1 << dims

    def bit(dim, core):
        return 2 << ((dim + core) % dims)

    def hop(block, dim):
        pairs = [(d, d ^ bit(dim, d & 1)) for d in range(n_virt)]
        return lax.ppermute(block, "virt", pairs)

    def sibling(block):
        return lax.ppermute(block, "virt", [(d, d ^ 1) for d in range(n_virt)])

    def across(block, mask):
        return lax.ppermute(block, "occ", [(d, d ^ mask) for d in range(n_occ)])

    def origin(mask, core):
        return sum(bit(dim, core) for dim in range(dims) if mask >> dim & 1)

    core = me_virt & 1
    origins = [
        me_virt ^ jnp.where(core == 0, origin(m, 0), origin(m, 1)) for m in range(n_own)
    ] + [
        me_virt ^ 1 ^ jnp.where(core == 0, origin(m, 1), origin(m, 0)) for m in range(n_own)
    ]
    by_owner = eps_vir.reshape(n_virt, n_parts, part)
    vb = by_owner[jnp.stack(origins)].transpose(1, 0, 2).reshape(n_parts, 1, LANES)
    va = lax.dynamic_slice_in_dim(eps_vir, me_virt * width, width).reshape(width, 1)
    scalars = (me, group_sizes, orbital_order, eps_occ, va, vb)

    z_parts = (1, 2, 2)
    cuts = z_parts
    starts = [sum(cuts[:c]) * part for c in range(len(cuts) + 1)]
    sends = []
    token, send, first = stage(None, basis, *scalars[:3], n_occ, 0, starts[1], with_own=True)
    sends.append([send])
    blocks = {}

    def spread(name, block):
        held = blocks[name] = [block] + [None] * (2 * n_own - 1)
        held[n_own] = sibling(block)
        for dim in range(dims):
            held[1 << dim] = hop(block, dim)

    def relay(token, name, level):
        held = blocks[name]
        arrived = [m for m in range(1, n_own) if m.bit_count() == level]
        token, gated = gate(token, (), [held[m] for m in arrived])
        for m, block in zip(arrived, gated):
            held[m] = block
        for m in arrived:
            for dim in range(m.bit_length(), dims):
                held[m | 1 << dim] = hop(held[m], dim)
        for m in arrived:
            held[n_own + m] = sibling(held[m])
        return token

    crossing = []
    n_chunks = len(z_parts)

    def cross(token, c):
        token, gated = gate(token, (), sends[c])
        if len(gated) == 1:
            crossing.append([lax.all_to_all(gated[0], "occ", 0, 0, tiled=True)])
        else:
            crossing.append([across(block, mask) for mask, block in enumerate(gated, 1)])
        return token

    total, held = None, (False,) * n_parts

    def add(jobs, last=False):
        nonlocal token, total, held
        token, total, held = density(
            token, scalars, blocks["first"], chunks, total, held, jobs, last, cuts
        )

    def arrive(name):
        nonlocal token
        for level in range(2, dims + 1):
            token = relay(token, name, level)

    chunks = {}

    def collect(c):
        nonlocal token
        token, (block,) = join(token, me, crossing[c], 1)
        spread(c, block)
        chunks[c] = blocks[c]

    token = cross(token, 0)
    spread("first", first)
    for c in range(1, n_chunks):
        token, *send = stage(token, basis, *scalars[:3], n_occ, starts[c], starts[c + 1])
        sends.append(send)
    for c in range(1, n_chunks):
        token = cross(token, c)
    token, _ = gate(token, (va, vb))
    collect(0)
    token = relay(token, "first", 1)
    arrive("first")
    token = relay(token, 0, 1)
    collect(1)
    arrive(0)
    early = cuts[0] + cuts[1]
    add([(0, early, (0,))])
    token = relay(token, 1, 1)
    collect(2)
    arrive(1)
    add([(0, n_parts, (1,)), (early, n_parts, (0, 2))])
    token = relay(token, 2, 1)
    add([(0, early, (2,))])
    arrive(2)
    add([(0, n_parts, (3, 4))], True)
    return total.reshape(1, CAP, width, n_occ * aux)


def solution(mesh):
    return jax.shard_map(
        on_device,
        mesh=mesh,
        in_specs=(P(None, "virt", "occ"), P(), P(), P(), P()),
        out_specs=P("occ", None, "virt", None),
        check_vma=False,
    )
```
